768 devices in a mesh: space: 64 (over z_hi, y, core), ens: 12 (over z_lo, x).
Axes of the slice: x: 4, y: 8, z: 12 (z_hi: 4, z_lo: 3; z = z_hi * 3 + z_lo), core: 2. Of those that a mesh axis runs over, the one named last changes fastest.
Arguments:
- members: bfloat16 [96, 8, 196608], P('ens', None, 'space'), may hold values from -6 to 6
- field: bfloat16 [8, 196608], P(None, 'space'), may hold values from -6 to 6
- weight: bfloat16 [1536, 4, 128, 128], P('space'), may hold values from -0.25 to 0.25
- offsets: int32 [1536, 4], P('space'), may hold values from -2 to 2
Outputs:
- increment: float32 [8, 196608], P(None, 'space')
The draws below stay inside these ranges and needn't reach their ends.
All inputs are finite; a program needn't handle non-finite values.
Results may differ from the reference program's by a relative error of at most 0.00077.
Values may be sent and summed in bfloat16 or wider, within the bound.
A program may use at most 32 MiB of HBM per device.

```python
import jax
import jax.numpy as jnp

CH = 8
BS = 128
HALO = 2
TAPS = 4
NB = 24
MEM = 96
NBLK = 1536
CELLS = 196608
N_SPACE = 64


def set_ends(array, key, low, largest):
    place = [jax.random.randint(jax.random.fold_in(key, axis), (), 0, length) for axis, length in enumerate(array.shape)]
    main_axis = array.shape.index(max(array.shape))
    beside = place[:main_axis] + [(place[main_axis] + 1) % array.shape[main_axis]] + place[main_axis + 1:]
    return array.at[tuple(place)].set(low).at[tuple(beside)].set(largest)


def level_of(stream_key, dims, cuts, low, largest):
    level, own = 1.0, jax.random.fold_in(stream_key, 6)
    for position, shards_of in cuts:
        draws = jnp.exp(jax.random.uniform(jax.random.fold_in(own, position), (shards_of,), jnp.float32, low / len(cuts), largest / len(cuts)))
        level = level * jnp.repeat(draws, dims[position] // shards_of).reshape([-1 if axis == position else 1 for axis in range(len(dims))])
    return level


def centred(key, extent, width, limit, pieces=(), kind=jnp.bfloat16):
    values = width * jax.random.normal(key, extent, jnp.float32)
    if pieces:
        values = values * level_of(key, extent, pieces, -0.22, 0.18)
    return jnp.clip(values, -limit, limit).astype(kind)


def setup_inputs(seed: int = 0) -> dict:
    key_of = jax.random.split(jax.random.key(seed), 5)
    members = centred(key_of[0], (MEM, CH, CELLS), 1.0, 6.0, ((0, 12), (2, 64)))
    field = centred(key_of[1], (CH, CELLS), 1.0, 6.0, ((1, 64),))
    weight = centred(key_of[2], (NBLK, TAPS, BS, BS), (TAPS * BS) ** -0.5, 0.25, ((0, 64),))
    offsets = set_ends(jax.random.randint(key_of[3], (NBLK, TAPS), -HALO, HALO + 1), jax.random.fold_in(key_of[3], 1), -HALO, HALO).astype(jnp.int32)
    return {"members": members, "field": field, "weight": weight, "offsets": offsets}


def reference(members, field, weight, offsets):
    row_total = MEM * CH
    block_total = NB * N_SPACE
    scaled = (members.astype(jnp.float32) * field.astype(jnp.float32)[None]).astype(jnp.bfloat16)
    scaled = scaled.reshape(row_total, block_total, BS).astype(jnp.float32)
    blocks = jnp.arange(block_total, dtype=jnp.int32)
    back = jnp.zeros((row_total, block_total, BS), jnp.float32)
    for tap_index in range(TAPS):
        source = ((blocks + offsets[:, tap_index]) % block_total).astype(jnp.int32)
        product = jnp.einsum("rbd,bcd->rbc", scaled, weight[:, tap_index].astype(jnp.float32))
        back = back.at[:, source].add(product)
    spread = back.astype(jnp.bfloat16).astype(jnp.float32)
    ahead = jnp.zeros((row_total, block_total, BS), jnp.float32)
    for tap_index in range(TAPS):
        source = ((blocks + offsets[:, tap_index]) % block_total).astype(jnp.int32)
        ahead = ahead + jnp.einsum("rbc,bcd->rbd", spread[:, source], weight[:, tap_index].astype(jnp.float32))
    ahead = ahead.reshape(MEM, CH, block_total * BS)
    return jnp.sum(members.astype(jnp.float32) * ahead, axis=0)
```

```python
import functools

import jax
import jax.numpy as jnp
from jax import lax
from jax.experimental import pallas as pl
from jax.experimental.pallas import tpu as pltpu
from jax.sharding import PartitionSpec as P

BS = 128
HALO = 2
TAPS = 4
RIM = 2 * HALO
MESH = pl.DeviceIdType.MESH


def kernel(
    n_space, n_ens, nb, rows, ch,
    offsets_ref, members_hbm, field_hbm, weight_hbm, out_ref,
    members, field, weight, back, spread, rim_out, rim_in, part, parts_in,
    in_sems, weight_sems, rim_send, rim_recv, rs_send, rs_recv, ag_send, ag_recv,
):
    me_s = lax.axis_index("space")
    me_e = lax.axis_index("ens")
    right = lax.rem(me_s + 1, n_space)
    left = lax.rem(me_s + n_space - 1, n_space)
    chunks = nb // RIM
    order = [0, chunks - 1] + list(range(1, chunks - 1))

    members_copy = pltpu.make_async_copy(members_hbm, members, in_sems.at[0])
    field_copy = pltpu.make_async_copy(field_hbm, field, in_sems.at[1])
    members_copy.start()
    field_copy.start()
    weight_copies = {}
    for c in order:
        piece = pl.ds(c * RIM, RIM)
        weight_copies[c] = pltpu.make_async_copy(weight_hbm.at[piece], weight.at[piece], weight_sems.at[c])
        weight_copies[c].start()

    barrier = pltpu.get_barrier_semaphore()
    for neighbour in (left, right):
        pl.semaphore_signal(barrier, inc=1, device_id=(neighbour, me_e), device_id_type=MESH)

    def greet(k, _):
        pl.semaphore_signal(barrier, inc=1, device_id=(me_s, lax.rem(me_e + k, n_ens)), device_id_type=MESH)
        return 0

    lax.fori_loop(1, n_ens, greet, 0)

    back[...] = jnp.zeros_like(back)

    def cells(b):
        return pl.ds(pl.multiple_of(b * BS, BS), BS)

    def adjoint(b, _):
        m = members[:, cells(b)].astype(jnp.float32).reshape(rows // ch, ch, BS)
        f = field[:, cells(b)].astype(jnp.float32)
        scaled = (m * f[None]).astype(jnp.bfloat16).reshape(rows, BS)
        product = lax.dot_general(
            scaled, weight[b], (((1,), (1,)), ((), ())), preferred_element_type=jnp.float32
        )
        taps = [offsets_ref[t, b] for t in range(TAPS)]
        for reach in range(-HALO, HALO + 1):
            slab = None
            for t in range(TAPS):
                term = jnp.where(taps[t] == reach, product[:, t * BS : (t + 1) * BS], 0.0)
                slab = term if slab is None else slab + term
            back[b + HALO + reach] += slab
        return 0

    def forward(b, _):
        total = None
        for t in range(TAPS):
            source = spread[b + HALO + offsets_ref[t, b]]
            term = jnp.dot(source, weight[b, t * BS : (t + 1) * BS, :], preferred_element_type=jnp.float32)
            total = term if total is None else total + term
        m = members[:, cells(b)].astype(jnp.float32).reshape(rows // ch, ch, BS)
        return jnp.sum(m * total.reshape(rows // ch, ch, BS), axis=0)

    def forward_pair(p):
        part[p, 0] = forward(2 * p, 0)
        part[p, 1] = forward(2 * p + 1, 0)

        @pl.when(p != me_e)
        def _():
            slot = lax.rem(p - me_e + n_ens, n_ens) - 1
            pltpu.make_async_remote_copy(
                src_ref=part.at[p], dst_ref=parts_in.at[slot],
                send_sem=rs_send, recv_sem=rs_recv,
                device_id=(me_s, p), device_id_type=MESH,
            ).start()

    members_copy.wait()
    field_copy.wait()
    weight_copies[0].wait()
    lax.fori_loop(0, RIM, adjoint, 0)
    rim_out[0] = back[0:RIM].astype(jnp.bfloat16)
    weight_copies[chunks - 1].wait()
    lax.fori_loop(nb - RIM, nb, adjoint, 0)
    rim_out[1] = back[nb : nb + RIM].astype(jnp.bfloat16)

    pl.semaphore_wait(barrier, n_ens + 1)
    rims = []
    for side, target in ((0, left), (1, right)):
        copy = pltpu.make_async_remote_copy(
            src_ref=rim_out.at[side], dst_ref=rim_in.at[side],
            send_sem=rim_send.at[side], recv_sem=rim_recv.at[side],
            device_id=(target, me_e), device_id_type=MESH,
        )
        copy.start()
        rims.append(copy)

    for c in range(1, chunks - 1):
        weight_copies[c].wait()
        lax.fori_loop(c * RIM, (c + 1) * RIM, adjoint, 0)

    spread[RIM:nb] = back[RIM:nb].astype(jnp.bfloat16)

    def inner(p, _):
        forward_pair(p)
        return 0

    lax.fori_loop(RIM // 2, (nb - RIM) // 2, inner, 0)

    rims[0].wait()
    rims[1].wait()
    spread[0:RIM] = (back[0:RIM] + rim_in[1].astype(jnp.float32)).astype(jnp.bfloat16)
    spread[nb : nb + RIM] = (back[nb : nb + RIM] + rim_in[0].astype(jnp.float32)).astype(jnp.bfloat16)
    lax.fori_loop(0, RIM // 2, inner, 0)
    lax.fori_loop((nb - RIM) // 2, nb // 2, inner, 0)

    all_in = pltpu.make_async_copy(parts_in, parts_in, rs_recv)
    all_in.wait()
    total = part[me_e]
    for k in range(n_ens - 1):
        total = total + parts_in[k]
    width = 2 * BS
    mine = pl.ds(pl.multiple_of(me_e * width, width), width)
    out_ref[:, mine] = jnp.concatenate([total[0], total[1]], axis=1)

    def give(k, _):
        pltpu.make_async_remote_copy(
            src_ref=out_ref.at[:, mine], dst_ref=out_ref.at[:, mine],
            send_sem=ag_send, recv_sem=ag_recv,
            device_id=(me_s, lax.rem(me_e + k, n_ens)), device_id_type=MESH,
        ).start()
        return 0

    lax.fori_loop(1, n_ens, give, 0)
    pltpu.make_async_copy(parts_in, parts_in, ag_recv).wait()
    pltpu.make_async_copy(parts_in, parts_in, rs_send).wait()
    pltpu.make_async_copy(parts_in, parts_in, ag_send).wait()


def local(n_space, n_ens, members, field, weight, offsets):
    member_count, ch, cell_total = members.shape
    nb = weight.shape[0]
    rows = member_count * ch
    dma = pltpu.SemaphoreType.DMA
    call = pl.pallas_call(
        functools.partial(kernel, n_space, n_ens, nb, rows, ch),
        out_shape=jax.ShapeDtypeStruct((ch, cell_total), jnp.float32),
        in_specs=[
            pl.BlockSpec(memory_space=pltpu.SMEM),
            pl.BlockSpec(memory_space=pl.ANY),
            pl.BlockSpec(memory_space=pl.ANY),
            pl.BlockSpec(memory_space=pl.ANY),
        ],
        out_specs=pl.BlockSpec(memory_space=pltpu.VMEM),
        scratch_shapes=[
            pltpu.VMEM((rows, cell_total), jnp.bfloat16),
            pltpu.VMEM((ch, cell_total), jnp.bfloat16),
            pltpu.VMEM((nb, TAPS * BS, BS), jnp.bfloat16),
            pltpu.VMEM((nb + RIM, rows, BS), jnp.float32),
            pltpu.VMEM((nb + RIM, rows, BS), jnp.bfloat16),
            pltpu.VMEM((2, RIM, rows, BS), jnp.bfloat16),
            pltpu.VMEM((2, RIM, rows, BS), jnp.bfloat16),
            pltpu.VMEM((n_ens, 2, ch, BS), jnp.float32),
            pltpu.VMEM((n_ens - 1, 2, ch, BS), jnp.float32),
            dma((2,)),
            dma((nb // RIM,)),
            dma((2,)),
            dma((2,)),
            dma,
            dma,
            dma,
            dma,
        ],
        compiler_params=pltpu.CompilerParams(
            collective_id=0, has_side_effects=True, vmem_limit_bytes=63 * 1024 * 1024
        ),
        cost_estimate=pl.CostEstimate(flops=403_000_000, bytes_accessed=3_800_000, transcendentals=0),
    )
    return call(
        offsets.T,
        members.reshape(rows, cell_total),
        field,
        weight.reshape(nb, TAPS * BS, BS),
    )


def solution(mesh):
    in_specs = (
        P("ens", None, "space"),
        P(None, "space"),
        P("space", None, None, None),
        P("space", None),
    )
    out_specs = P(None, "space")
    body = functools.partial(local, mesh.shape["space"], mesh.shape["ens"])
    return jax.shard_map(body, mesh=mesh, in_specs=in_specs, out_specs=out_specs, check_vma=False)
```

```python
import functools

import jax
import jax.numpy as jnp
from jax import lax
from jax.experimental import pallas as pl
from jax.experimental.pallas import tpu as pltpu
from jax.sharding import PartitionSpec as P

BS = 128
HALO = 2
TAPS = 4
RIM = 2 * HALO
VMEM_LIMIT = 32 * 1024 * 1024
MESH = pl.DeviceIdType.MESH


def kernel(
    n_space, n_ens, nb, rows, ch,
    offsets_ref, members_hbm, field_hbm, weight_hbm, out_ref,
    members, field, weight, back, spread, rim_out, rim_in, part, parts_in,
    in_sems, weight_sems, rim_send, rim_recv, rs_send, rs_recv, ag_send, ag_recv,
):
    me_s = lax.axis_index("space")
    me_e = lax.axis_index("ens")
    right = lax.rem(me_s + 1, n_space)
    left = lax.rem(me_s + n_space - 1, n_space)
    chunks = nb // RIM
    order = [0, chunks - 1] + list(range(1, chunks - 1))

    members_copy = pltpu.make_async_copy(members_hbm, members, in_sems.at[0])
    field_copy = pltpu.make_async_copy(field_hbm, field, in_sems.at[1])
    members_copy.start()
    field_copy.start()
    weight_copies = {}
    for c in order:
        piece = pl.ds(c * RIM, RIM)
        weight_copies[c] = pltpu.make_async_copy(weight_hbm.at[piece], weight.at[piece], weight_sems.at[c])
        weight_copies[c].start()

    barrier = pltpu.get_barrier_semaphore()
    for neighbour in (left, right):
        pl.semaphore_signal(barrier, inc=1, device_id=(neighbour, me_e), device_id_type=MESH)

    def greet(k, _):
        pl.semaphore_signal(barrier, inc=1, device_id=(me_s, lax.rem(me_e + k, n_ens)), device_id_type=MESH)
        return 0

    lax.fori_loop(1, n_ens, greet, 0)

    back[...] = jnp.zeros_like(back)

    def cells(b):
        return pl.ds(b * BS, BS)

    def adjoint(b):
        m = members[:, cells(b)].astype(jnp.float32).reshape(rows // ch, ch, BS)
        f = field[:, cells(b)].astype(jnp.float32)
        scaled = (m * f[None]).astype(jnp.bfloat16).reshape(rows, BS)
        product = lax.dot_general(
            scaled, weight[b], (((1,), (1,)), ((), ())), preferred_element_type=jnp.float32
        )
        taps = [offsets_ref[t, b] for t in range(TAPS)]
        for reach in range(-HALO, HALO + 1):
            slab = None
            for t in range(TAPS):
                term = jnp.where(taps[t] == reach, product[:, t * BS : (t + 1) * BS], 0.0)
                slab = term if slab is None else slab + term
            back[b + HALO + reach] += slab

    def forward(b):
        total = None
        for t in range(TAPS):
            source = spread[b + HALO + offsets_ref[t, b]]
            term = jnp.dot(source, weight[b, t * BS : (t + 1) * BS, :], preferred_element_type=jnp.float32)
            total = term if total is None else total + term
        m = members[:, cells(b)].astype(jnp.float32).reshape(rows // ch, ch, BS)
        return jnp.sum(m * total.reshape(rows // ch, ch, BS), axis=0)

    def forward_pair(p):
        part[p, 0] = forward(2 * p)
        part[p, 1] = forward(2 * p + 1)

        @pl.when(p != me_e)
        def _():
            slot = lax.rem(p - me_e + n_ens, n_ens) - 1
            pltpu.make_async_remote_copy(
                src_ref=part.at[p], dst_ref=parts_in.at[slot],
                send_sem=rs_send, recv_sem=rs_recv,
                device_id=(me_s, p), device_id_type=MESH,
            ).start()

    members_copy.wait()
    field_copy.wait()
    weight_copies[0].wait()
    for b in range(RIM):
        adjoint(b)
    rim_out[0] = back[0:RIM].astype(jnp.bfloat16)
    weight_copies[chunks - 1].wait()
    for b in range(nb - RIM, nb):
        adjoint(b)
    rim_out[1] = back[nb : nb + RIM].astype(jnp.bfloat16)

    pl.semaphore_wait(barrier, n_ens + 1)
    rims = []
    for side, target in ((0, left), (1, right)):
        copy = pltpu.make_async_remote_copy(
            src_ref=rim_out.at[side], dst_ref=rim_in.at[side],
            send_sem=rim_send.at[side], recv_sem=rim_recv.at[side],
            device_id=(target, me_e), device_id_type=MESH,
        )
        copy.start()
        rims.append(copy)

    for c in range(1, chunks - 1):
        weight_copies[c].wait()
        for b in range(c * RIM, (c + 1) * RIM):
            adjoint(b)

    spread[RIM:nb] = back[RIM:nb].astype(jnp.bfloat16)

    for p in range(RIM // 2, (nb - RIM) // 2):
        forward_pair(p)

    rims[0].wait()
    rims[1].wait()
    spread[0:RIM] = (back[0:RIM] + rim_in[1].astype(jnp.float32)).astype(jnp.bfloat16)
    spread[nb : nb + RIM] = (back[nb : nb + RIM] + rim_in[0].astype(jnp.float32)).astype(jnp.bfloat16)
    for p in (*range(RIM // 2), *range((nb - RIM) // 2, nb // 2)):
        forward_pair(p)

    all_in = pltpu.make_async_copy(parts_in, parts_in, rs_recv)
    all_in.wait()
    total = part[me_e]
    for k in range(n_ens - 1):
        total = total + parts_in[k]
    width = 2 * BS
    mine = pl.ds(pl.multiple_of(me_e * width, width), width)
    out_ref[:, mine] = jnp.concatenate([total[0], total[1]], axis=1)

    def give(k, _):
        pltpu.make_async_remote_copy(
            src_ref=out_ref.at[:, mine], dst_ref=out_ref.at[:, mine],
            send_sem=ag_send, recv_sem=ag_recv,
            device_id=(me_s, lax.rem(me_e + k, n_ens)), device_id_type=MESH,
        ).start()
        return 0

    lax.fori_loop(1, n_ens, give, 0)
    pltpu.make_async_copy(parts_in, parts_in, ag_recv).wait()
    pltpu.make_async_copy(parts_in, parts_in, rs_send).wait()
    pltpu.make_async_copy(parts_in, parts_in, ag_send).wait()


def local(n_space, n_ens, members, field, weight, offsets):
    member_count, ch, cell_total = members.shape
    nb = weight.shape[0]
    rows = member_count * ch
    dma = pltpu.SemaphoreType.DMA
    call = pl.pallas_call(
        functools.partial(kernel, n_space, n_ens, nb, rows, ch),
        out_shape=pltpu.VMEM((ch, cell_total), jnp.float32),
        in_specs=[
            pl.BlockSpec(memory_space=pltpu.SMEM),
            pl.BlockSpec(memory_space=pltpu.HBM),
            pl.BlockSpec(memory_space=pltpu.HBM),
            pl.BlockSpec(memory_space=pltpu.HBM),
        ],
        out_specs=pl.BlockSpec(memory_space=pltpu.VMEM),
        scratch_shapes=[
            pltpu.VMEM((rows, cell_total), jnp.bfloat16),
            pltpu.VMEM((ch, cell_total), jnp.bfloat16),
            pltpu.VMEM((nb, TAPS * BS, BS), jnp.bfloat16),
            pltpu.VMEM((nb + RIM, rows, BS), jnp.float32),
            pltpu.VMEM((nb + RIM, rows, BS), jnp.bfloat16),
            pltpu.VMEM((2, RIM, rows, BS), jnp.bfloat16),
            pltpu.VMEM((2, RIM, rows, BS), jnp.bfloat16),
            pltpu.VMEM((n_ens, 2, ch, BS), jnp.float32),
            pltpu.VMEM((n_ens - 1, 2, ch, BS), jnp.float32),
            dma((2,)),
            dma((nb // RIM,)),
            dma((2,)),
            dma((2,)),
            dma,
            dma,
            dma,
            dma,
        ],
        compiler_params=pltpu.CompilerParams(
            collective_id=0, has_side_effects=True, vmem_limit_bytes=VMEM_LIMIT
        ),
        cost_estimate=pl.CostEstimate(flops=403_000_000, bytes_accessed=3_800_000, transcendentals=0),
    )
    return call(
        pltpu.with_memory_space_constraint(offsets.T, pltpu.HBM),
        pltpu.with_memory_space_constraint(members.reshape(rows, cell_total), pltpu.HBM),
        pltpu.with_memory_space_constraint(field, pltpu.HBM),
        pltpu.with_memory_space_constraint(weight.reshape(nb, TAPS * BS, BS), pltpu.HBM),
    )


def solution(mesh):
    in_specs = (
        P("ens", None, "space"),
        P(None, "space"),
        P("space", None, None, None),
        P("space", None),
    )
    out_specs = P(None, "space")
    body = functools.partial(local, mesh.shape["space"], mesh.shape["ens"])
    return jax.shard_map(body, mesh=mesh, in_specs=in_specs, out_specs=out_specs, check_vma=False)
```

```python
import functools

import jax
import jax.numpy as jnp
from jax import lax
from jax.experimental import pallas as pl
from jax.experimental.pallas import tpu as pltpu
from jax.sharding import PartitionSpec as P

BS = 128
HALO = 2
TAPS = 4
RIM = 2 * HALO
ROW = 4
MESH = pl.DeviceIdType.MESH
VMEM_LIMIT = 32 * 1024 * 1024


def kernel(
    n_space, n_ens, nb, rows, ch,
    offsets_hbm, members_hbm, field_hbm, weight_hbm, out_ref,
    offsets, members, field, weight, back, spread, rim_out, rim_in, part, parts_in, border,
    in_sems, weight_sems, ready, rim_send, rim_recv, rs_send, rs_recv, ag_send, ag_recv, border_send, border_recv,
):
    me_s = lax.axis_index("space")
    me_e = lax.axis_index("ens")
    right = lax.rem(me_s + 1, n_space)
    left = lax.rem(me_s + n_space - 1, n_space)
    first = me_s == 0
    last = me_s == n_space - 1
    chunks = nb // RIM
    inner = chunks - 2
    order = [0, chunks - 1] + list(range(1, chunks - 1))

    partners = []
    for dx in (2, 1, 3, 0):
        for dz in (1, 2, 0):
            if dx or dz:
                z = lax.rem(me_e // ROW + dz, n_ens // ROW)
                partners.append(z * ROW + lax.rem(lax.rem(me_e, ROW) + dx, ROW))

    def owner(g):
        return ROW + g

    loads = [
        pltpu.make_async_copy(members_hbm, members, in_sems.at[0]),
        pltpu.make_async_copy(field_hbm, field, in_sems.at[1]),
        pltpu.make_async_copy(offsets_hbm, offsets, in_sems.at[2]),
    ]
    for copy in loads:
        copy.start()
    weight_copies = {}
    for c in order:
        piece = pl.ds(c * RIM, RIM)
        weight_copies[c] = pltpu.make_async_copy(weight_hbm.at[piece], weight.at[piece], weight_sems.at[c])
        weight_copies[c].start()

    barrier = pltpu.get_barrier_semaphore()

    @pl.when(jnp.logical_not(last))
    def _():
        pl.semaphore_signal(barrier, inc=1, device_id=(right, me_e), device_id_type=MESH)

    @pl.when(first)
    def _():
        pl.semaphore_signal(barrier, inc=1, device_id=(left, me_e), device_id_type=MESH)

    for p in partners:
        pl.semaphore_signal(barrier, inc=1, device_id=(me_s, p), device_id_type=MESH)

    back[...] = jnp.zeros_like(back)

    def cells(b):
        return pl.ds(b * BS if isinstance(b, int) else pl.multiple_of(b * BS, BS), BS)

    def adjoint(b):
        m = members[:, cells(b)].astype(jnp.float32).reshape(rows // ch, ch, BS)
        f = field[:, cells(b)].astype(jnp.float32)
        scaled = (m * f[None]).astype(jnp.bfloat16).reshape(rows, BS)
        product = lax.dot_general(
            scaled, weight[b], (((1,), (1,)), ((), ())), preferred_element_type=jnp.float32
        )
        taps = [offsets[t, b] for t in range(TAPS)]
        for reach in range(-HALO, HALO + 1):
            slab = None
            for t in range(TAPS):
                term = jnp.where(taps[t] == reach, product[:, t * BS : (t + 1) * BS], 0.0)
                slab = term if slab is None else slab + term
            back[b + HALO + reach] += slab

    def forward(b):
        total = None
        for t in range(TAPS):
            source = spread[b + HALO + offsets[t, b]]
            term = jnp.dot(source, weight[b, t * BS : (t + 1) * BS, :], preferred_element_type=jnp.float32)
            total = term if total is None else total + term
        m = members[:, cells(b)].astype(jnp.float32).reshape(rows // ch, ch, BS)
        return jnp.sum(m * total.reshape(rows // ch, ch, BS), axis=0)

    def send_rim(side):
        pltpu.make_async_remote_copy(
            src_ref=rim_out.at[side], dst_ref=rim_in.at[1 - side],
            send_sem=rim_send.at[side], recv_sem=rim_recv.at[1 - side],
            device_id=(right if side else left, me_e), device_id_type=MESH,
        ).start()

    def wait_for(ref, sem):
        pltpu.make_async_copy(ref, ref, sem).wait()

    for copy in loads:
        copy.wait()
    weight_copies[0].wait()
    for b in range(RIM):
        adjoint(b)
    rim_out[0] = back[0:RIM].astype(jnp.bfloat16)
    weight_copies[chunks - 1].wait()
    for b in range(nb - RIM, nb):
        adjoint(b)
    rim_out[1] = back[nb : nb + RIM].astype(jnp.bfloat16)

    pl.semaphore_wait(barrier, n_ens - 1 + jnp.where(first, 0, 1) + jnp.where(last, 1, 0))

    @pl.when(jnp.logical_not(first))
    def _():
        send_rim(0)
        pl.semaphore_signal(ready.at[1], inc=1, device_id=(left, me_e), device_id_type=MESH)

    @pl.when(last)
    def _():
        send_rim(1)
        pl.semaphore_signal(ready.at[0], inc=1, device_id=(right, me_e), device_id_type=MESH)

    for c in range(1, chunks - 1):
        weight_copies[c].wait()
        for b in range(c * RIM, (c + 1) * RIM):
            adjoint(b)

    spread[RIM:nb] = back[RIM:nb].astype(jnp.bfloat16)

    for g in range(inner):
        for i in range(RIM):
            part[g, i] = forward(RIM * (g + 1) + i)

        @pl.when(me_e != owner(g))
        def _():
            slot = lax.rem(owner(g) - me_e + n_ens, n_ens) - 1
            pltpu.make_async_remote_copy(
                src_ref=part.at[g], dst_ref=parts_in.at[slot],
                send_sem=rs_send.at[g], recv_sem=rs_recv,
                device_id=(me_s, owner(g)), device_id_type=MESH,
            ).start()

    @pl.when(jnp.logical_not(last))
    def _():
        pl.semaphore_wait(ready.at[1], 1)
        send_rim(1)

    def finish_border(side):
        base = side * (nb - RIM)
        rim = pl.ds(side * nb, RIM)
        wait_for(rim_in.at[side], rim_recv.at[side])
        spread[rim] = (back[rim] + rim_in[side].astype(jnp.float32)).astype(jnp.bfloat16)
        for i in range(RIM):
            border[side, me_e, i] = forward(base + i)
        for p in partners:
            pltpu.make_async_remote_copy(
                src_ref=border.at[side, me_e], dst_ref=border.at[side, me_e],
                send_sem=border_send.at[side], recv_sem=border_recv.at[side],
                device_id=(me_s, p), device_id_type=MESH,
            ).start()

    near = 1 - lax.rem(me_s, 2)
    far = 1 - near
    finish_border(near)

    @pl.when(first)
    def _():
        pl.semaphore_wait(ready.at[0], 1)
        send_rim(0)

    width = RIM * BS
    owns = jnp.logical_and(me_e >= owner(0), me_e < owner(inner))

    @pl.when(owns)
    def _():
        wait_for(parts_in, rs_recv)
        g = me_e - owner(0)
        total = part[g]
        for k in range(n_ens - 1):
            total = total + parts_in[k]
        mine = pl.ds(pl.multiple_of((g + 1) * width, width), width)
        out_ref[:, mine] = jnp.concatenate([total[i] for i in range(RIM)], axis=1)
        for p in partners:
            pltpu.make_async_remote_copy(
                src_ref=out_ref.at[:, mine], dst_ref=out_ref.at[:, mine],
                send_sem=ag_send, recv_sem=ag_recv.at[g],
                device_id=(me_s, p), device_id_type=MESH,
            ).start()

    finish_border(far)

    for side in (0, 1):
        wait_for(border.at[side, 0 : n_ens - 1], border_recv.at[side])
        total = border[side, 0]
        for k in range(1, n_ens):
            total = total + border[side, k]
        start = side * (nb - RIM) * BS
        out_ref[:, start : start + width] = jnp.concatenate([total[i] for i in range(RIM)], axis=1)

    for g in range(inner):

        @pl.when(me_e != owner(g))
        def _():
            wait_for(out_ref.at[:, pl.ds((g + 1) * width, width)], ag_recv.at[g])
            wait_for(part.at[g], rs_send.at[g])

    @pl.when(owns)
    def _():
        wait_for(parts_in, ag_send)

    for side in (0, 1):
        wait_for(rim_out.at[side], rim_send.at[side])
        wait_for(border.at[side, 0 : n_ens - 1], border_send.at[side])


def local(n_space, n_ens, members, field, weight, offsets):
    member_count, ch, cell_total = members.shape
    nb = weight.shape[0]
    rows = member_count * ch
    inner = nb // RIM - 2
    dma = pltpu.SemaphoreType.DMA
    call = pl.pallas_call(
        functools.partial(kernel, n_space, n_ens, nb, rows, ch),
        out_shape=pltpu.VMEM((ch, cell_total), jnp.float32),
        in_specs=[pl.BlockSpec(memory_space=pltpu.HBM)] * 4,
        out_specs=pl.BlockSpec(memory_space=pltpu.VMEM),
        scratch_shapes=[
            pltpu.SMEM((TAPS, nb), jnp.int32),
            pltpu.VMEM((rows, cell_total), jnp.bfloat16),
            pltpu.VMEM((ch, cell_total), jnp.bfloat16),
            pltpu.VMEM((nb, TAPS * BS, BS), jnp.bfloat16),
            pltpu.VMEM((nb + RIM, rows, BS), jnp.float32),
            pltpu.VMEM((nb + RIM, rows, BS), jnp.bfloat16),
            pltpu.VMEM((2, RIM, rows, BS), jnp.bfloat16),
            pltpu.VMEM((2, RIM, rows, BS), jnp.bfloat16),
            pltpu.VMEM((inner, RIM, ch, BS), jnp.float32),
            pltpu.VMEM((n_ens - 1, RIM, ch, BS), jnp.float32),
            pltpu.VMEM((2, n_ens, RIM, ch, BS), jnp.float32),
            dma((3,)),
            dma((nb // RIM,)),
            pltpu.SemaphoreType.REGULAR((2,)),
            dma((2,)),
            dma((2,)),
            dma((inner,)),
            dma,
            dma,
            dma((inner,)),
            dma((2,)),
            dma((2,)),
        ],
        compiler_params=pltpu.CompilerParams(
            collective_id=0, has_side_effects=True, vmem_limit_bytes=VMEM_LIMIT
        ),
        cost_estimate=pl.CostEstimate(flops=403_000_000, bytes_accessed=3_800_000, transcendentals=0),
    )
    operands = (
        offsets.T,
        members.reshape(rows, cell_total),
        field,
        weight.reshape(nb, TAPS * BS, BS),
    )
    return call(*(pltpu.with_memory_space_constraint(x, pltpu.HBM) for x in operands))


def solution(mesh):
    in_specs = (
        P("ens", None, "space"),
        P(None, "space"),
        P("space", None, None, None),
        P("space", None),
    )
    out_specs = P(None, "space")
    body = functools.partial(local, mesh.shape["space"], mesh.shape["ens"])
    return jax.shard_map(body, mesh=mesh, in_specs=in_specs, out_specs=out_specs, check_vma=False)
```

```python
import functools

import jax
import jax.numpy as jnp
from jax import lax
from jax.experimental import pallas as pl
from jax.experimental.pallas import tpu as pltpu
from jax.sharding import PartitionSpec as P

BS = 128
HALO = 2
TAPS = 4
RIM = 2 * HALO
ROW = 4
MESH = pl.DeviceIdType.MESH
VMEM_LIMIT = 32 * 1024 * 1024


def kernel(
    n_space, n_ens, nb, rows, ch,
    offsets_hbm, members_hbm, field_hbm, weight_hbm, out_ref,
    offsets, members, field, weight, back, spread, rim_out, rim_in, part, parts_in, border,
    in_sems, weight_sems, ready, met, rim_send, rim_recv, rs_send, rs_recv, ag_send, ag_recv, border_send, border_recv,
):
    me_s = lax.axis_index("space")
    me_e = lax.axis_index("ens")
    right = lax.rem(me_s + 1, n_space)
    left = lax.rem(me_s + n_space - 1, n_space)
    first = me_s == 0
    last = me_s == n_space - 1
    chunks = nb // RIM
    inner = chunks - 2
    order = [chunks - 1, 0] + list(range(1, chunks - 1))

    row, x = me_e // ROW, lax.rem(me_e, ROW)
    away = jnp.where(row == 0, 2, 1)
    partners = []
    for dz in (away, n_ens // ROW - away, 0):
        for dx in (2, 1, 3, 0):
            if dx or not isinstance(dz, int):
                partners.append(lax.rem(row + dz, n_ens // ROW) * ROW + lax.rem(x + dx, ROW))
    cross = [row * ROW + lax.rem(x + dx, ROW) for dx in range(1, ROW)]
    cross += [lax.rem(row + dz, n_ens // ROW) * ROW + x for dz in range(1, n_ens // ROW)]

    def owner(g):
        return ROW + g

    loads = [
        pltpu.make_async_copy(members_hbm, members, in_sems.at[0]),
        pltpu.make_async_copy(field_hbm, field, in_sems.at[1]),
        pltpu.make_async_copy(offsets_hbm, offsets, in_sems.at[2]),
    ]
    for copy in loads:
        copy.start()
    weight_copies = {}
    for c in order:
        piece = pl.ds(c * RIM, RIM)
        weight_copies[c] = pltpu.make_async_copy(weight_hbm.at[piece], weight.at[piece], weight_sems.at[c])
        weight_copies[c].start()

    barrier = pltpu.get_barrier_semaphore()

    @pl.when(jnp.logical_not(last))
    def _():
        pl.semaphore_signal(barrier, inc=1, device_id=(right, me_e), device_id_type=MESH)

    @pl.when(first)
    def _():
        pl.semaphore_signal(barrier, inc=1, device_id=(left, me_e), device_id_type=MESH)

    for p in cross:
        pl.semaphore_signal(barrier, inc=1, device_id=(me_s, p), device_id_type=MESH)

    back[...] = jnp.zeros_like(back)

    def cells(b):
        return pl.ds(b * BS if isinstance(b, int) else pl.multiple_of(b * BS, BS), BS)

    def adjoint(b):
        m = members[:, cells(b)].astype(jnp.float32).reshape(rows // ch, ch, BS)
        f = field[:, cells(b)].astype(jnp.float32)
        scaled = (m * f[None]).astype(jnp.bfloat16).reshape(rows, BS)
        product = lax.dot_general(
            scaled, weight[b], (((1,), (1,)), ((), ())), preferred_element_type=jnp.float32
        )
        taps = [offsets[t, b] for t in range(TAPS)]
        for reach in range(-HALO, HALO + 1):
            slab = None
            for t in range(TAPS):
                term = jnp.where(taps[t] == reach, product[:, t * BS : (t + 1) * BS], 0.0)
                slab = term if slab is None else slab + term
            back[b + HALO + reach] += slab

    def forward(b):
        total = None
        for t in range(TAPS):
            source = spread[b + HALO + offsets[t, b]]
            term = jnp.dot(source, weight[b, t * BS : (t + 1) * BS, :], preferred_element_type=jnp.float32)
            total = term if total is None else total + term
        m = members[:, cells(b)].astype(jnp.float32).reshape(rows // ch, ch, BS)
        return jnp.sum(m * total.reshape(rows // ch, ch, BS), axis=0)

    def send_rim(side):
        pltpu.make_async_remote_copy(
            src_ref=rim_out.at[side], dst_ref=rim_in.at[1 - side],
            send_sem=rim_send.at[side], recv_sem=rim_recv.at[1 - side],
            device_id=(right if side else left, me_e), device_id_type=MESH,
        ).start()

    def wait_for(ref, sem):
        pltpu.make_async_copy(ref, ref, sem).wait()

    for copy in loads:
        copy.wait()
    weight_copies[chunks - 1].wait()
    for b in range(nb - RIM, nb):
        adjoint(b)
    rim_out[1] = back[nb : nb + RIM].astype(jnp.bfloat16)
    weight_copies[0].wait()
    for b in range(RIM):
        adjoint(b)
    rim_out[0] = back[0:RIM].astype(jnp.bfloat16)

    pl.semaphore_wait(barrier, len(cross) + jnp.where(first, 0, 1) + jnp.where(last, 1, 0))

    @pl.when(jnp.logical_not(first))
    def _():
        send_rim(0)
        pl.semaphore_signal(ready.at[1], inc=1, device_id=(left, me_e), device_id_type=MESH)

    @pl.when(last)
    def _():
        send_rim(1)
        pl.semaphore_signal(ready.at[0], inc=1, device_id=(right, me_e), device_id_type=MESH)

    for p in cross:
        pl.semaphore_signal(met, inc=1, device_id=(me_s, p), device_id_type=MESH)

    for c in range(1, chunks - 1):
        weight_copies[c].wait()
        for b in range(c * RIM, (c + 1) * RIM):
            adjoint(b)

    spread[RIM:nb] = back[RIM:nb].astype(jnp.bfloat16)

    pl.semaphore_wait(met, len(cross))
    for g in range(inner):
        for i in range(RIM):
            part[g, i] = forward(RIM * (g + 1) + i)

        @pl.when(me_e != owner(g))
        def _():
            slot = lax.rem(owner(g) - me_e + n_ens, n_ens) - 1
            pltpu.make_async_remote_copy(
                src_ref=part.at[g], dst_ref=parts_in.at[slot],
                send_sem=rs_send.at[g], recv_sem=rs_recv,
                device_id=(me_s, owner(g)), device_id_type=MESH,
            ).start()

    @pl.when(jnp.logical_not(last))
    def _():
        pl.semaphore_wait(ready.at[1], 1)
        send_rim(1)

    def finish_border(side):
        base = side * (nb - RIM)
        rim = pl.ds(side * nb, RIM)
        wait_for(rim_in.at[side], rim_recv.at[side])
        spread[rim] = (back[rim] + rim_in[side].astype(jnp.float32)).astype(jnp.bfloat16)
        for i in range(RIM):
            border[side, me_e, i] = forward(base + i)
        for p in partners:
            pltpu.make_async_remote_copy(
                src_ref=border.at[side, me_e], dst_ref=border.at[side, me_e],
                send_sem=border_send.at[side], recv_sem=border_recv.at[side],
                device_id=(me_s, p), device_id_type=MESH,
            ).start()

    near = 1 - lax.rem(me_s, 2)
    far = 1 - near
    finish_border(near)

    width = RIM * BS
    owns = jnp.logical_and(me_e >= owner(0), me_e < owner(inner))

    @pl.when(owns)
    def _():
        wait_for(parts_in, rs_recv)
        g = me_e - owner(0)
        total = part[g]
        for k in range(n_ens - 1):
            total = total + parts_in[k]
        mine = pl.ds(pl.multiple_of((g + 1) * width, width), width)
        out_ref[:, mine] = jnp.concatenate([total[i] for i in range(RIM)], axis=1)
        for p in partners:
            pltpu.make_async_remote_copy(
                src_ref=out_ref.at[:, mine], dst_ref=out_ref.at[:, mine],
                send_sem=ag_send, recv_sem=ag_recv.at[g],
                device_id=(me_s, p), device_id_type=MESH,
            ).start()

    @pl.when(first)
    def _():
        pl.semaphore_wait(ready.at[0], 1)
        send_rim(0)

    finish_border(far)

    def sum_border(side):
        wait_for(border.at[side, 0 : n_ens - 1], border_recv.at[side])
        total = border[side, 0]
        for k in range(1, n_ens):
            total = total + border[side, k]
        columns = pl.ds(pl.multiple_of(side * (nb - RIM) * BS, width), width)
        out_ref[:, columns] = jnp.concatenate([total[i] for i in range(RIM)], axis=1)
        wait_for(border.at[side, 0 : n_ens - 1], border_send.at[side])

    sum_border(near)
    for g in range(inner):

        @pl.when(me_e != owner(g))
        def _():
            wait_for(out_ref.at[:, pl.ds((g + 1) * width, width)], ag_recv.at[g])
            wait_for(part.at[g], rs_send.at[g])

    @pl.when(owns)
    def _():
        wait_for(parts_in, ag_send)

    for side in (0, 1):
        wait_for(rim_out.at[side], rim_send.at[side])
    sum_border(far)


def local(n_space, n_ens, members, field, weight, offsets):
    member_count, ch, cell_total = members.shape
    nb = weight.shape[0]
    rows = member_count * ch
    inner = nb // RIM - 2
    dma = pltpu.SemaphoreType.DMA
    call = pl.pallas_call(
        functools.partial(kernel, n_space, n_ens, nb, rows, ch),
        out_shape=pltpu.VMEM((ch, cell_total), jnp.float32),
        in_specs=[pl.BlockSpec(memory_space=pltpu.HBM)] * 4,
        out_specs=pl.BlockSpec(memory_space=pltpu.VMEM),
        scratch_shapes=[
            pltpu.SMEM((TAPS, nb), jnp.int32),
            pltpu.VMEM((rows, cell_total), jnp.bfloat16),
            pltpu.VMEM((ch, cell_total), jnp.bfloat16),
            pltpu.VMEM((nb, TAPS * BS, BS), jnp.bfloat16),
            pltpu.VMEM((nb + RIM, rows, BS), jnp.float32),
            pltpu.VMEM((nb + RIM, rows, BS), jnp.bfloat16),
            pltpu.VMEM((2, RIM, rows, BS), jnp.bfloat16),
            pltpu.VMEM((2, RIM, rows, BS), jnp.bfloat16),
            pltpu.VMEM((inner, RIM, ch, BS), jnp.float32),
            pltpu.VMEM((n_ens - 1, RIM, ch, BS), jnp.float32),
            pltpu.VMEM((2, n_ens, RIM, ch, BS), jnp.float32),
            dma((3,)),
            dma((nb // RIM,)),
            pltpu.SemaphoreType.REGULAR((2,)),
            pltpu.SemaphoreType.REGULAR,
            dma((2,)),
            dma((2,)),
            dma((inner,)),
            dma,
            dma,
            dma((inner,)),
            dma((2,)),
            dma((2,)),
        ],
        compiler_params=pltpu.CompilerParams(
            collective_id=0, has_side_effects=True, vmem_limit_bytes=VMEM_LIMIT
        ),
        cost_estimate=pl.CostEstimate(flops=403_000_000, bytes_accessed=3_800_000, transcendentals=0),
    )
    operands = (
        offsets.T,
        members.reshape(rows, cell_total),
        field,
        weight.reshape(nb, TAPS * BS, BS),
    )
    return call(*(pltpu.with_memory_space_constraint(x, pltpu.HBM) for x in operands))


def solution(mesh):
    in_specs = (
        P("ens", None, "space"),
        P(None, "space"),
        P("space", None, None, None),
        P("space", None),
    )
    out_specs = P(None, "space")
    body = functools.partial(local, mesh.shape["space"], mesh.shape["ens"])
    return jax.shard_map(body, mesh=mesh, in_specs=in_specs, out_specs=out_specs, check_vma=False)
```

```python
import functools

import jax
import jax.numpy as jnp
from jax import lax
from jax.experimental import pallas as pl
from jax.experimental.pallas import tpu as pltpu
from jax.sharding import PartitionSpec as P

BS = 128
HALO = 2
TAPS = 4
RIM = 2 * HALO
ROW = 4
MESH = pl.DeviceIdType.MESH
VMEM_LIMIT = 32 * 1024 * 1024


def kernel(
    n_space, n_ens, nb, rows, ch,
    offsets_hbm, members_hbm, field_hbm, weight_hbm, out_ref,
    offsets, members, field, weight, back, spread, rim_out, rim_in, part, parts_in, border,
    in_sems, member_sems, weight_sems, ready, met, rim_send, rim_recv, rs_send, rs_recv, ag_send, ag_recv, border_send, border_recv,
):
    me_s = lax.axis_index("space")
    me_e = lax.axis_index("ens")
    right = lax.rem(me_s + 1, n_space)
    left = lax.rem(me_s + n_space - 1, n_space)
    first = me_s == 0
    last = me_s == n_space - 1
    ends = jnp.logical_or(first, last)
    tail = me_s >= n_space - 2
    chunks = nb // RIM
    inner = chunks - 2
    order = [chunks - 1, 0] + list(range(1, chunks - 1))

    row, x = me_e // ROW, lax.rem(me_e, ROW)
    away = jnp.where(row == 0, 2, 1)
    partners = []
    for dz in (away, n_ens // ROW - away, 0):
        for dx in (2, 1, 3, 0):
            if dx or not isinstance(dz, int):
                partners.append(lax.rem(row + dz, n_ens // ROW) * ROW + lax.rem(x + dx, ROW))
    cross = [row * ROW + lax.rem(x + dx, ROW) for dx in range(1, ROW)]
    cross += [lax.rem(row + dz, n_ens // ROW) * ROW + x for dz in range(1, n_ens // ROW)]

    def owner(g):
        return ROW + g

    loads = [
        pltpu.make_async_copy(offsets_hbm, offsets, in_sems.at[2]),
        pltpu.make_async_copy(field_hbm, field, in_sems.at[1]),
    ]
    for copy in loads:
        copy.start()
    member_copies, weight_copies = {}, {}
    pieces = {chunks - 1: (chunks - 1, chunks), 0: (0, 1), 1: (1, chunks - 1)}
    for c in order:
        if c in pieces:
            low, high = pieces[c]
            columns = pl.ds(low * RIM * BS, (high - low) * RIM * BS)
            member_copies[c] = pltpu.make_async_copy(members_hbm.at[:, columns], members.at[:, columns], member_sems.at[len(member_copies)])
        piece = pl.ds(c * RIM, RIM)
        weight_copies[c] = pltpu.make_async_copy(weight_hbm.at[piece], weight.at[piece], weight_sems.at[c])

    def load(c):
        if c in member_copies:
            member_copies[c].start()
        weight_copies[c].start()

    load(chunks - 1)
    load(0)

    barrier = pltpu.get_barrier_semaphore()

    @pl.when(jnp.logical_not(tail))
    def _():
        pl.semaphore_signal(barrier, inc=1, device_id=(right, me_e), device_id_type=MESH)

    @pl.when(ends)
    def _():
        pl.semaphore_signal(barrier, inc=1, device_id=(left, me_e), device_id_type=MESH)

    for p in cross:
        pl.semaphore_signal(barrier, inc=1, device_id=(me_s, p), device_id_type=MESH)

    back[...] = jnp.zeros_like(back)

    def cells(b):
        return pl.ds(b * BS if isinstance(b, int) else pl.multiple_of(b * BS, BS), BS)

    def adjoint(b):
        m = members[:, cells(b)].astype(jnp.float32).reshape(rows // ch, ch, BS)
        f = field[:, cells(b)].astype(jnp.float32)
        scaled = (m * f[None]).astype(jnp.bfloat16).reshape(rows, BS)
        product = lax.dot_general(
            scaled, weight[b], (((1,), (1,)), ((), ())), preferred_element_type=jnp.float32
        )
        taps = [offsets[t, b] for t in range(TAPS)]
        for reach in range(-HALO, HALO + 1):
            slab = None
            for t in range(TAPS):
                term = jnp.where(taps[t] == reach, product[:, t * BS : (t + 1) * BS], 0.0)
                slab = term if slab is None else slab + term
            back[b + HALO + reach] += slab

    def forward(b):
        total = None
        for t in range(TAPS):
            source = spread[b + HALO + offsets[t, b]]
            term = jnp.dot(source, weight[b, t * BS : (t + 1) * BS, :], preferred_element_type=jnp.float32)
            total = term if total is None else total + term
        m = members[:, cells(b)].astype(jnp.float32).reshape(rows // ch, ch, BS)
        return jnp.sum(m * total.reshape(rows // ch, ch, BS), axis=0)

    def send_rim(side):
        pltpu.make_async_remote_copy(
            src_ref=rim_out.at[side], dst_ref=rim_in.at[1 - side],
            send_sem=rim_send.at[side], recv_sem=rim_recv.at[1 - side],
            device_id=(right if side else left, me_e), device_id_type=MESH,
        ).start()

    def wait_for(ref, sem):
        pltpu.make_async_copy(ref, ref, sem).wait()

    for copy in loads:
        copy.wait()
    member_copies[chunks - 1].wait()
    weight_copies[chunks - 1].wait()
    for c in order[2:]:
        load(c)
    for b in range(nb - RIM, nb):
        adjoint(b)
    rim_out[1] = back[nb : nb + RIM].astype(jnp.bfloat16)
    pl.semaphore_wait(barrier, len(cross) + jnp.where(ends, 0, 1) + jnp.where(tail, 1, 0))

    @pl.when(tail)
    def _():
        send_rim(1)
        pl.semaphore_signal(ready.at[0], inc=1, device_id=(right, me_e), device_id_type=MESH)

    member_copies[0].wait()
    weight_copies[0].wait()
    for b in range(RIM):
        adjoint(b)
    rim_out[0] = back[0:RIM].astype(jnp.bfloat16)

    @pl.when(jnp.logical_not(ends))
    def _():
        send_rim(0)
        pl.semaphore_signal(ready.at[1], inc=1, device_id=(left, me_e), device_id_type=MESH)

    for p in cross:
        pl.semaphore_signal(met, inc=1, device_id=(me_s, p), device_id_type=MESH)

    for c in range(1, chunks - 1):
        if c in member_copies:
            member_copies[c].wait()
        weight_copies[c].wait()
        for b in range(c * RIM, (c + 1) * RIM):
            adjoint(b)

    spread[RIM:nb] = back[RIM:nb].astype(jnp.bfloat16)

    pl.semaphore_wait(met, len(cross))
    for g in range(inner):
        for i in range(RIM):
            part[g, i] = forward(RIM * (g + 1) + i)

        @pl.when(me_e != owner(g))
        def _():
            slot = lax.rem(owner(g) - me_e + n_ens, n_ens) - 1
            pltpu.make_async_remote_copy(
                src_ref=part.at[g], dst_ref=parts_in.at[slot],
                send_sem=rs_send.at[g], recv_sem=rs_recv,
                device_id=(me_s, owner(g)), device_id_type=MESH,
            ).start()

    @pl.when(jnp.logical_not(tail))
    def _():
        pl.semaphore_wait(ready.at[1], 1)
        send_rim(1)

    def finish_border(side):
        base = side * (nb - RIM)
        rim = pl.ds(side * nb, RIM)
        wait_for(rim_in.at[side], rim_recv.at[side])
        spread[rim] = (back[rim] + rim_in[side].astype(jnp.float32)).astype(jnp.bfloat16)
        for i in range(RIM):
            border[side, me_e, i] = forward(base + i)
        for p in partners:
            pltpu.make_async_remote_copy(
                src_ref=border.at[side, me_e], dst_ref=border.at[side, me_e],
                send_sem=border_send.at[side], recv_sem=border_recv.at[side],
                device_id=(me_s, p), device_id_type=MESH,
            ).start()

    @pl.when(last)
    def _():
        pl.semaphore_wait(ready.at[0], 1)
        send_rim(0)

    near = 1 - lax.rem(me_s, 2)
    far = 1 - near
    finish_border(near)

    width = RIM * BS
    owns = jnp.logical_and(me_e >= owner(0), me_e < owner(inner))

    @pl.when(owns)
    def _():
        wait_for(parts_in, rs_recv)
        g = me_e - owner(0)
        total = part[g]
        for k in range(n_ens - 1):
            total = total + parts_in[k]
        mine = pl.ds(pl.multiple_of((g + 1) * width, width), width)
        out_ref[:, mine] = jnp.concatenate([total[i] for i in range(RIM)], axis=1)
        for p in partners:
            pltpu.make_async_remote_copy(
                src_ref=out_ref.at[:, mine], dst_ref=out_ref.at[:, mine],
                send_sem=ag_send, recv_sem=ag_recv.at[g],
                device_id=(me_s, p), device_id_type=MESH,
            ).start()

    @pl.when(first)
    def _():
        pl.semaphore_wait(ready.at[0], 1)
        send_rim(0)

    finish_border(far)

    def sum_border(side):
        wait_for(border.at[side, 0 : n_ens - 1], border_recv.at[side])
        total = border[side, 0]
        for k in range(1, n_ens):
            total = total + border[side, k]
        columns = pl.ds(pl.multiple_of(side * (nb - RIM) * BS, width), width)
        out_ref[:, columns] = jnp.concatenate([total[i] for i in range(RIM)], axis=1)
        wait_for(border.at[side, 0 : n_ens - 1], border_send.at[side])

    sum_border(near)
    for g in range(inner):

        @pl.when(me_e != owner(g))
        def _():
            wait_for(out_ref.at[:, pl.ds((g + 1) * width, width)], ag_recv.at[g])
            wait_for(part.at[g], rs_send.at[g])

    @pl.when(owns)
    def _():
        wait_for(parts_in, ag_send)

    for side in (0, 1):
        wait_for(rim_out.at[side], rim_send.at[side])
    sum_border(far)


def local(n_space, n_ens, members, field, weight, offsets):
    member_count, ch, cell_total = members.shape
    nb = weight.shape[0]
    rows = member_count * ch
    inner = nb // RIM - 2
    dma = pltpu.SemaphoreType.DMA
    call = pl.pallas_call(
        functools.partial(kernel, n_space, n_ens, nb, rows, ch),
        out_shape=pltpu.VMEM((ch, cell_total), jnp.float32),
        in_specs=[pl.BlockSpec(memory_space=pltpu.HBM)] * 4,
        out_specs=pl.BlockSpec(memory_space=pltpu.VMEM),
        scratch_shapes=[
            pltpu.SMEM((TAPS, nb), jnp.int32),
            pltpu.VMEM((rows, cell_total), jnp.bfloat16),
            pltpu.VMEM((ch, cell_total), jnp.bfloat16),
            pltpu.VMEM((nb, TAPS * BS, BS), jnp.bfloat16),
            pltpu.VMEM((nb + RIM, rows, BS), jnp.float32),
            pltpu.VMEM((nb + RIM, rows, BS), jnp.bfloat16),
            pltpu.VMEM((2, RIM, rows, BS), jnp.bfloat16),
            pltpu.VMEM((2, RIM, rows, BS), jnp.bfloat16),
            pltpu.VMEM((inner, RIM, ch, BS), jnp.float32),
            pltpu.VMEM((n_ens - 1, RIM, ch, BS), jnp.float32),
            pltpu.VMEM((2, n_ens, RIM, ch, BS), jnp.float32),
            dma((3,)),
            dma((3,)),
            dma((nb // RIM,)),
            pltpu.SemaphoreType.REGULAR((2,)),
            pltpu.SemaphoreType.REGULAR,
            dma((2,)),
            dma((2,)),
            dma((inner,)),
            dma,
            dma,
            dma((inner,)),
            dma((2,)),
            dma((2,)),
        ],
        compiler_params=pltpu.CompilerParams(
            collective_id=0, has_side_effects=True, vmem_limit_bytes=VMEM_LIMIT
        ),
        cost_estimate=pl.CostEstimate(flops=403_000_000, bytes_accessed=3_800_000, transcendentals=0),
    )
    operands = (
        offsets.T,
        members.reshape(rows, cell_total),
        field,
        weight.reshape(nb, TAPS * BS, BS),
    )
    return call(*(pltpu.with_memory_space_constraint(x, pltpu.HBM) for x in operands))


def solution(mesh):
    in_specs = (
        P("ens", None, "space"),
        P(None, "space"),
        P("space", None, None, None),
        P("space", None),
    )
    out_specs = P(None, "space")
    body = functools.partial(local, mesh.shape["space"], mesh.shape["ens"])
    return jax.shard_map(body, mesh=mesh, in_specs=in_specs, out_specs=out_specs, check_vma=False)
```

```python
import functools

import jax
import jax.numpy as jnp
from jax import lax
from jax.experimental import pallas as pl
from jax.experimental.pallas import tpu as pltpu
from jax.sharding import PartitionSpec as P

BS = 128
HALO = 2
TAPS = 4
RIM = 2 * HALO
ROW = 4
MESH = pl.DeviceIdType.MESH
VMEM_LIMIT = 32 * 1024 * 1024


def kernel(
    n_space, n_ens, nb, rows, ch,
    offsets_hbm, members_hbm, field_hbm, weight_hbm, out_ref,
    offsets, members, field, weight, back, spread, rim_out, rim_in, part, parts_in, border,
    rims, pack, gift_members, gift_spread, gift_back,
    in_sems, member_sems, weight_sems, ready, met, rim_send, rim_recv, rs_send, rs_recv, ag_send, ag_recv, border_send, border_recv,
    rims_recv, gift_send, gift_recv,
):
    me_s = lax.axis_index("space")
    me_e = lax.axis_index("ens")
    right = lax.rem(me_s + 1, n_space)
    left = lax.rem(me_s + n_space - 1, n_space)
    first = me_s == 0
    last = me_s == n_space - 1
    ends = jnp.logical_or(first, last)
    tail = me_s >= n_space - 2
    chunks = nb // RIM
    inner = chunks - 2
    order = [chunks - 1, 0] + list(range(1, chunks - 1))

    row, x = me_e // ROW, lax.rem(me_e, ROW)
    away = jnp.where(row == 0, 2, 1)
    partners = []
    for dz in (away, n_ens // ROW - away, 0):
        for dx in (2, 1, 3, 0):
            if dx or not isinstance(dz, int):
                partners.append(lax.rem(row + dz, n_ens // ROW) * ROW + lax.rem(x + dx, ROW))
    cross = [row * ROW + lax.rem(x + dx, ROW) for dx in range(1, ROW)]
    cross += [lax.rem(row + dz, n_ens // ROW) * ROW + x for dz in range(1, n_ens // ROW)]

    n_rows = n_ens // ROW
    giver = jnp.logical_and(first, row > 0)
    taker = jnp.logical_and(first, row == 0)

    def owner(g):
        return ROW + g

    loads = [
        pltpu.make_async_copy(offsets_hbm, offsets, in_sems.at[2]),
        pltpu.make_async_copy(field_hbm, field, in_sems.at[1]),
    ]
    for copy in loads:
        copy.start()
    member_copies, weight_copies = {}, {}
    pieces = {chunks - 1: (chunks - 1, chunks), 0: (0, 1), 1: (1, chunks - 1)}
    for c in order:
        if c in pieces:
            low, high = pieces[c]
            columns = pl.ds(low * RIM * BS, (high - low) * RIM * BS)
            member_copies[c] = pltpu.make_async_copy(members_hbm.at[:, columns], members.at[:, columns], member_sems.at[len(member_copies)])
        piece = pl.ds(c * RIM, RIM)
        weight_copies[c] = pltpu.make_async_copy(weight_hbm.at[piece], weight.at[piece], weight_sems.at[c])

    def load(c):
        if c in member_copies:
            member_copies[c].start()
        weight_copies[c].start()

    load(chunks - 1)
    load(0)

    barrier = pltpu.get_barrier_semaphore()

    @pl.when(jnp.logical_not(tail))
    def _():
        pl.semaphore_signal(barrier, inc=1, device_id=(right, me_e), device_id_type=MESH)

    @pl.when(ends)
    def _():
        pl.semaphore_signal(barrier, inc=1, device_id=(left, me_e), device_id_type=MESH)

    @pl.when(taker)
    def _():
        for r in range(1, n_rows):
            pl.semaphore_signal(barrier, inc=1, device_id=(left, r * ROW + x), device_id_type=MESH)

    for p in cross:
        pl.semaphore_signal(barrier, inc=1, device_id=(me_s, p), device_id_type=MESH)

    back[...] = jnp.zeros_like(back)

    def cells(b):
        return pl.ds(b * BS if isinstance(b, int) else pl.multiple_of(b * BS, BS), BS)

    def adjoint(b):
        m = members[:, cells(b)].astype(jnp.float32).reshape(rows // ch, ch, BS)
        f = field[:, cells(b)].astype(jnp.float32)
        scaled = (m * f[None]).astype(jnp.bfloat16).reshape(rows, BS)
        product = lax.dot_general(
            scaled, weight[b], (((1,), (1,)), ((), ())), preferred_element_type=jnp.float32
        )
        taps = [offsets[t, b] for t in range(TAPS)]
        for reach in range(-HALO, HALO + 1):
            slab = None
            for t in range(TAPS):
                term = jnp.where(taps[t] == reach, product[:, t * BS : (t + 1) * BS], 0.0)
                slab = term if slab is None else slab + term
            back[b + HALO + reach] += slab

    def forward(b):
        total = None
        for t in range(TAPS):
            source = spread[b + HALO + offsets[t, b]]
            term = jnp.dot(source, weight[b, t * BS : (t + 1) * BS, :], preferred_element_type=jnp.float32)
            total = term if total is None else total + term
        m = members[:, cells(b)].astype(jnp.float32).reshape(rows // ch, ch, BS)
        return jnp.sum(m * total.reshape(rows // ch, ch, BS), axis=0)

    def send_rim(side):
        pltpu.make_async_remote_copy(
            src_ref=rim_out.at[side], dst_ref=rim_in.at[1 - side],
            send_sem=rim_send.at[side], recv_sem=rim_recv.at[1 - side],
            device_id=(right if side else left, me_e), device_id_type=MESH,
        ).start()

    def wait_for(ref, sem):
        pltpu.make_async_copy(ref, ref, sem).wait()

    for copy in loads:
        copy.wait()
    member_copies[chunks - 1].wait()
    weight_copies[chunks - 1].wait()
    for c in order[2:]:
        load(c)
    for b in range(nb - RIM, nb):
        adjoint(b)
    rim_out[1] = back[nb : nb + RIM].astype(jnp.bfloat16)
    pl.semaphore_wait(barrier, len(cross) + jnp.where(ends, 0, 1) + jnp.where(tail, 1, 0)
        + jnp.where(jnp.logical_and(last, row > 0), 1, 0))

    @pl.when(tail)
    def _():
        @pl.when(last)
        def _():
            pltpu.make_async_remote_copy(
                src_ref=rim_out.at[1], dst_ref=rims.at[row],
                send_sem=rim_send.at[1], recv_sem=rims_recv.at[row],
                device_id=(right, x), device_id_type=MESH,
            ).start()

        @pl.when(jnp.logical_not(last))
        def _():
            send_rim(1)

        pl.semaphore_signal(ready.at[0], inc=1, device_id=(right, me_e), device_id_type=MESH)

    member_copies[0].wait()
    weight_copies[0].wait()
    for b in range(RIM):
        adjoint(b)
    rim_out[0] = back[0:RIM].astype(jnp.bfloat16)

    @pl.when(jnp.logical_not(ends))
    def _():
        send_rim(0)
        pl.semaphore_signal(ready.at[1], inc=1, device_id=(left, me_e), device_id_type=MESH)

    for p in cross:
        pl.semaphore_signal(met, inc=1, device_id=(me_s, p), device_id_type=MESH)

    @pl.when(first)
    def _():
        pl.semaphore_wait(ready.at[1], 1)
        send_rim(1)

    gifts = (
        (pack, gift_members),
        (spread.at[RIM : 2 * RIM], gift_spread),
        (rim_out.at[0], gift_back),
    )

    @pl.when(giver)
    def _():
        for b in range(RIM):
            pack[b] = members[:, cells(b)]
        for i, (mine, gift) in ((0, gifts[0]), (2, gifts[2])):
            pltpu.make_async_remote_copy(
                src_ref=mine, dst_ref=gift.at[row - 1],
                send_sem=gift_send.at[i], recv_sem=gift_recv.at[i, row - 1],
                device_id=(me_s, x), device_id_type=MESH,
            ).start()

    for c in range(1, chunks - 1):
        if c in member_copies:
            member_copies[c].wait()
        weight_copies[c].wait()
        for b in range(c * RIM, (c + 1) * RIM):
            adjoint(b)

    spread[RIM:nb] = back[RIM:nb].astype(jnp.bfloat16)

    @pl.when(giver)
    def _():
        pltpu.make_async_remote_copy(
            src_ref=gifts[1][0], dst_ref=gift_spread.at[row - 1],
            send_sem=gift_send.at[1], recv_sem=gift_recv.at[1, row - 1],
            device_id=(me_s, x), device_id_type=MESH,
        ).start()

    pl.semaphore_wait(met, len(cross))
    for g in range(inner):
        for i in range(RIM):
            part[g, i] = forward(RIM * (g + 1) + i)

        @pl.when(me_e != owner(g))
        def _():
            slot = lax.rem(owner(g) - me_e + n_ens, n_ens) - 1
            pltpu.make_async_remote_copy(
                src_ref=part.at[g], dst_ref=parts_in.at[slot],
                send_sem=rs_send.at[g], recv_sem=rs_recv,
                device_id=(me_s, owner(g)), device_id_type=MESH,
            ).start()

    @pl.when(jnp.logical_not(jnp.logical_or(first, tail)))
    def _():
        pl.semaphore_wait(ready.at[1], 1)
        send_rim(1)

    def finish_border(side):
        base = side * (nb - RIM)
        rim = pl.ds(side * nb, RIM)
        wait_for(rim_in.at[side], rim_recv.at[side])
        spread[rim] = (back[rim] + rim_in[side].astype(jnp.float32)).astype(jnp.bfloat16)
        for i in range(RIM):
            border[side, me_e, i] = forward(base + i)
        give_border(side)

    def give_border(side):
        for p in partners:
            pltpu.make_async_remote_copy(
                src_ref=border.at[side, me_e], dst_ref=border.at[side, me_e],
                send_sem=border_send.at[side], recv_sem=border_recv.at[side],
                device_id=(me_s, p), device_id_type=MESH,
            ).start()

    @pl.when(last)
    def _():
        pl.semaphore_wait(ready.at[0], 1)
        send_rim(0)

    near = 1 - lax.rem(me_s, 2)
    far = 1 - near
    finish_border(near)

    width = RIM * BS
    owns = jnp.logical_and(me_e >= owner(0), me_e < owner(inner))

    @pl.when(owns)
    def _():
        wait_for(parts_in, rs_recv)
        g = me_e - owner(0)
        total = part[g]
        for k in range(n_ens - 1):
            total = total + parts_in[k]
        mine = pl.ds(pl.multiple_of((g + 1) * width, width), width)
        out_ref[:, mine] = jnp.concatenate([total[i] for i in range(RIM)], axis=1)
        for p in partners:
            pltpu.make_async_remote_copy(
                src_ref=out_ref.at[:, mine], dst_ref=out_ref.at[:, mine],
                send_sem=ag_send, recv_sem=ag_recv.at[g],
                device_id=(me_s, p), device_id_type=MESH,
            ).start()

    @pl.when(first)
    def _():
        pl.semaphore_wait(ready.at[0], 1)
        send_rim(0)

    @pl.when(jnp.logical_not(first))
    def _():
        finish_border(far)

    @pl.when(taker)
    def _():
        def finish_row(r, _):
            wait_for(rims.at[r], rims_recv.at[r])

            @pl.when(r > 0)
            def _():
                for i, (mine, gift) in enumerate(gifts):
                    wait_for(gift.at[r - 1], gift_recv.at[i, r - 1])
                for b in range(RIM):
                    members[:, cells(b)] = gift_members[r - 1, b]
                spread[RIM : 2 * RIM] = gift_spread[r - 1]
                back[0:RIM] = gift_back[r - 1].astype(jnp.float32)

            spread[0:RIM] = (back[0:RIM] + rims[r].astype(jnp.float32)).astype(jnp.bfloat16)
            for i in range(RIM):
                border[0, me_e, i] += forward(i)
            return 0

        border[0, me_e] = jnp.zeros_like(border[0, me_e])
        lax.fori_loop(0, n_rows, finish_row, 0)
        give_border(0)

    def sum_border(side, count=n_ens):
        total = border[side, 0]
        for k in range(1, count):
            total = total + border[side, k]
        columns = pl.ds(pl.multiple_of(side * (nb - RIM) * BS, width), width)
        out_ref[:, columns] = jnp.concatenate([total[i] for i in range(RIM)], axis=1)

    others = pl.ds(0, n_ens - 1)
    wait_for(border.at[near, others], border_recv.at[near])
    sum_border(near)
    wait_for(border.at[near, others], border_send.at[near])
    for g in range(inner):

        @pl.when(me_e != owner(g))
        def _():
            wait_for(out_ref.at[:, pl.ds((g + 1) * width, width)], ag_recv.at[g])
            wait_for(part.at[g], rs_send.at[g])

    @pl.when(owns)
    def _():
        wait_for(parts_in, ag_send)

    for side in (0, 1):
        wait_for(rim_out.at[side], rim_send.at[side])

    @pl.when(giver)
    def _():
        for i, (mine, gift) in enumerate(gifts):
            wait_for(gift.at[0], gift_send.at[i])
        wait_for(border.at[0, 0:ROW], border_recv.at[0])

    @pl.when(taker)
    def _():
        wait_for(border.at[0, 0 : ROW - 1], border_recv.at[0])

    @pl.when(first)
    def _():
        sum_border(0, ROW)

    @pl.when(taker)
    def _():
        wait_for(border.at[0, others], border_send.at[0])

    @pl.when(jnp.logical_not(first))
    def _():
        wait_for(border.at[far, others], border_recv.at[far])
        sum_border(far)
        wait_for(border.at[far, others], border_send.at[far])


def local(n_space, n_ens, members, field, weight, offsets):
    member_count, ch, cell_total = members.shape
    nb = weight.shape[0]
    rows = member_count * ch
    inner = nb // RIM - 2
    dma = pltpu.SemaphoreType.DMA
    call = pl.pallas_call(
        functools.partial(kernel, n_space, n_ens, nb, rows, ch),
        out_shape=pltpu.VMEM((ch, cell_total), jnp.float32),
        in_specs=[pl.BlockSpec(memory_space=pltpu.HBM)] * 4,
        out_specs=pl.BlockSpec(memory_space=pltpu.VMEM),
        scratch_shapes=[
            pltpu.SMEM((TAPS, nb), jnp.int32),
            pltpu.VMEM((rows, cell_total), jnp.bfloat16),
            pltpu.VMEM((ch, cell_total), jnp.bfloat16),
            pltpu.VMEM((nb, TAPS * BS, BS), jnp.bfloat16),
            pltpu.VMEM((nb + RIM, rows, BS), jnp.float32),
            pltpu.VMEM((nb + RIM, rows, BS), jnp.bfloat16),
            pltpu.VMEM((2, RIM, rows, BS), jnp.bfloat16),
            pltpu.VMEM((2, RIM, rows, BS), jnp.bfloat16),
            pltpu.VMEM((inner, RIM, ch, BS), jnp.float32),
            pltpu.VMEM((n_ens - 1, RIM, ch, BS), jnp.float32),
            pltpu.VMEM((2, n_ens, RIM, ch, BS), jnp.float32),
            pltpu.VMEM((n_ens // ROW, RIM, rows, BS), jnp.bfloat16),
            pltpu.VMEM((RIM, rows, BS), jnp.bfloat16),
            pltpu.VMEM((n_ens // ROW - 1, RIM, rows, BS), jnp.bfloat16),
            pltpu.VMEM((n_ens // ROW - 1, RIM, rows, BS), jnp.bfloat16),
            pltpu.VMEM((n_ens // ROW - 1, RIM, rows, BS), jnp.bfloat16),
            dma((3,)),
            dma((3,)),
            dma((nb // RIM,)),
            pltpu.SemaphoreType.REGULAR((2,)),
            pltpu.SemaphoreType.REGULAR,
            dma((2,)),
            dma((2,)),
            dma((inner,)),
            dma,
            dma,
            dma((inner,)),
            dma((2,)),
            dma((2,)),
            dma((n_ens // ROW,)),
            dma((3,)),
            dma((3, n_ens // ROW - 1)),
        ],
        compiler_params=pltpu.CompilerParams(
            collective_id=0, has_side_effects=True, vmem_limit_bytes=VMEM_LIMIT
        ),
        cost_estimate=pl.CostEstimate(flops=403_000_000, bytes_accessed=3_800_000, transcendentals=0),
    )
    operands = (
        offsets.T,
        members.reshape(rows, cell_total),
        field,
        weight.reshape(nb, TAPS * BS, BS),
    )
    return call(*(pltpu.with_memory_space_constraint(x, pltpu.HBM) for x in operands))


def solution(mesh):
    in_specs = (
        P("ens", None, "space"),
        P(None, "space"),
        P("space", None, None, None),
        P("space", None),
    )
    out_specs = P(None, "space")
    body = functools.partial(local, mesh.shape["space"], mesh.shape["ens"])
    return jax.shard_map(body, mesh=mesh, in_specs=in_specs, out_specs=out_specs, check_vma=False)
```

```python
import functools

import jax
import jax.numpy as jnp
from jax import lax
from jax.experimental import pallas as pl
from jax.experimental.pallas import tpu as pltpu
from jax.sharding import PartitionSpec as P

BS = 128
HALO = 2
TAPS = 4
RIM = 2 * HALO
ROW = 4
MESH = pl.DeviceIdType.MESH
VMEM_LIMIT = 32 * 1024 * 1024


def kernel(
    n_space, n_ens, nb, rows, ch,
    offsets_hbm, members_hbm, field_hbm, weight_hbm, out_ref,
    offsets, members, field, weight, back, spread, rim_out, rim_in, part, parts_in, border,
    rims, pack, gift_members, gift_spread, gift_back,
    in_sems, member_sems, weight_sems, ready, met, rim_send, rim_recv, rs_send, rs_recv, ag_send, ag_recv, border_send, border_recv,
    rims_recv, gift_send, gift_recv,
):
    me_s = lax.axis_index("space")
    me_e = lax.axis_index("ens")
    right = lax.rem(me_s + 1, n_space)
    left = lax.rem(me_s + n_space - 1, n_space)
    first = me_s == 0
    last = me_s == n_space - 1
    ends = jnp.logical_or(first, last)
    tail = me_s >= n_space - 2
    chunks = nb // RIM
    inner = chunks - 2
    order = [chunks - 1, 0] + list(range(1, chunks - 1))

    row, x = me_e // ROW, lax.rem(me_e, ROW)
    away = jnp.where(row == 0, 2, 1)
    partners = []
    for dz in (away, n_ens // ROW - away, 0):
        for dx in (2, 1, 3, 0):
            if dx or not isinstance(dz, int):
                partners.append(lax.rem(row + dz, n_ens // ROW) * ROW + lax.rem(x + dx, ROW))
    cross = [row * ROW + lax.rem(x + dx, ROW) for dx in range(1, ROW)]
    cross += [lax.rem(row + dz, n_ens // ROW) * ROW + x for dz in range(1, n_ens // ROW)]

    n_rows = n_ens // ROW
    giver = jnp.logical_and(first, row > 0)
    taker = jnp.logical_and(first, row == 0)

    def owner(g):
        return ROW + g

    loads = [
        pltpu.make_async_copy(offsets_hbm, offsets, in_sems.at[2]),
        pltpu.make_async_copy(field_hbm, field, in_sems.at[1]),
    ]
    for copy in loads:
        copy.start()
    member_copies, weight_copies = {}, {}
    pieces = {chunks - 1: (chunks - 1, chunks), 0: (0, 1), 1: (1, chunks - 1)}
    for c in order:
        if c in pieces:
            low, high = pieces[c]
            columns = pl.ds(low * RIM * BS, (high - low) * RIM * BS)
            member_copies[c] = pltpu.make_async_copy(members_hbm.at[:, columns], members.at[:, columns], member_sems.at[len(member_copies)])
        piece = pl.ds(c * RIM, RIM)
        weight_copies[c] = pltpu.make_async_copy(weight_hbm.at[piece], weight.at[piece], weight_sems.at[c])

    def load(c):
        if c in member_copies:
            member_copies[c].start()
        weight_copies[c].start()

    load(chunks - 1)
    load(0)

    barrier = pltpu.get_barrier_semaphore()

    @pl.when(jnp.logical_not(tail))
    def _():
        pl.semaphore_signal(barrier, inc=1, device_id=(right, me_e), device_id_type=MESH)

    @pl.when(ends)
    def _():
        pl.semaphore_signal(barrier, inc=1, device_id=(left, me_e), device_id_type=MESH)

    @pl.when(taker)
    def _():
        for r in range(1, n_rows):
            pl.semaphore_signal(barrier, inc=1, device_id=(left, r * ROW + x), device_id_type=MESH)

    for p in cross:
        pl.semaphore_signal(barrier, inc=1, device_id=(me_s, p), device_id_type=MESH)

    back[...] = jnp.zeros_like(back)

    def cells(b):
        return pl.ds(b * BS if isinstance(b, int) else pl.multiple_of(b * BS, BS), BS)

    def adjoint(b):
        m = members[:, cells(b)].astype(jnp.float32).reshape(rows // ch, ch, BS)
        f = field[:, cells(b)].astype(jnp.float32)
        scaled = (m * f[None]).astype(jnp.bfloat16).reshape(rows, BS)
        product = lax.dot_general(
            scaled, weight[b], (((1,), (1,)), ((), ())), preferred_element_type=jnp.float32
        )
        taps = [offsets[t, b] for t in range(TAPS)]
        for reach in range(-HALO, HALO + 1):
            slab = None
            for t in range(TAPS):
                term = jnp.where(taps[t] == reach, product[:, t * BS : (t + 1) * BS], 0.0)
                slab = term if slab is None else slab + term
            back[b + HALO + reach] += slab

    def forward(b):
        total = None
        for t in range(TAPS):
            source = spread[b + HALO + offsets[t, b]]
            term = jnp.dot(source, weight[b, t * BS : (t + 1) * BS, :], preferred_element_type=jnp.float32)
            total = term if total is None else total + term
        m = members[:, cells(b)].astype(jnp.float32).reshape(rows // ch, ch, BS)
        return jnp.sum(m * total.reshape(rows // ch, ch, BS), axis=0)

    def send_rim(side):
        pltpu.make_async_remote_copy(
            src_ref=rim_out.at[side], dst_ref=rim_in.at[1 - side],
            send_sem=rim_send.at[side], recv_sem=rim_recv.at[1 - side],
            device_id=(right if side else left, me_e), device_id_type=MESH,
        ).start()

    def wait_for(ref, sem):
        pltpu.make_async_copy(ref, ref, sem).wait()

    for copy in loads:
        copy.wait()
    member_copies[chunks - 1].wait()
    weight_copies[chunks - 1].wait()
    for c in order[2:]:
        load(c)
    for b in range(nb - RIM, nb):
        adjoint(b)
    rim_out[1] = back[nb : nb + RIM].astype(jnp.bfloat16)
    pl.semaphore_wait(barrier, len(cross) + jnp.where(ends, 0, 1) + jnp.where(tail, 1, 0)
        + jnp.where(jnp.logical_and(last, row > 0), 1, 0))

    @pl.when(tail)
    def _():
        @pl.when(last)
        def _():
            pltpu.make_async_remote_copy(
                src_ref=rim_out.at[1], dst_ref=rims.at[row],
                send_sem=rim_send.at[1], recv_sem=rims_recv.at[row],
                device_id=(right, x), device_id_type=MESH,
            ).start()

        @pl.when(jnp.logical_not(last))
        def _():
            send_rim(1)

        pl.semaphore_signal(ready.at[0], inc=1, device_id=(right, me_e), device_id_type=MESH)

    member_copies[0].wait()
    weight_copies[0].wait()
    for b in range(RIM):
        adjoint(b)
    rim_out[0] = back[0:RIM].astype(jnp.bfloat16)

    @pl.when(jnp.logical_not(ends))
    def _():
        send_rim(0)
        pl.semaphore_signal(ready.at[1], inc=1, device_id=(left, me_e), device_id_type=MESH)

    for p in cross:
        pl.semaphore_signal(met, inc=1, device_id=(me_s, p), device_id_type=MESH)

    @pl.when(first)
    def _():
        pl.semaphore_wait(ready.at[1], 1)
        send_rim(1)

    gifts = (
        (pack, gift_members),
        (spread.at[RIM : 2 * RIM], gift_spread),
        (rim_out.at[0], gift_back),
    )

    @pl.when(giver)
    def _():
        for b in range(RIM):
            pack[b] = members[:, cells(b)]
        for i, (mine, gift) in ((0, gifts[0]), (2, gifts[2])):
            pltpu.make_async_remote_copy(
                src_ref=mine, dst_ref=gift.at[row - 1],
                send_sem=gift_send.at[i], recv_sem=gift_recv.at[i, row - 1],
                device_id=(me_s, x), device_id_type=MESH,
            ).start()

    for c in range(1, chunks - 1):
        if c in member_copies:
            member_copies[c].wait()
        weight_copies[c].wait()
        for b in range(c * RIM, (c + 1) * RIM):
            adjoint(b)

    spread[RIM:nb] = back[RIM:nb].astype(jnp.bfloat16)

    @pl.when(giver)
    def _():
        pltpu.make_async_remote_copy(
            src_ref=gifts[1][0], dst_ref=gift_spread.at[row - 1],
            send_sem=gift_send.at[1], recv_sem=gift_recv.at[1, row - 1],
            device_id=(me_s, x), device_id_type=MESH,
        ).start()

    pl.semaphore_wait(met, len(cross))
    for g in range(inner):
        for i in range(RIM):
            part[g, i] = forward(RIM * (g + 1) + i)

        @pl.when(me_e != owner(g))
        def _():
            slot = lax.rem(owner(g) - me_e + n_ens, n_ens) - 1
            pltpu.make_async_remote_copy(
                src_ref=part.at[g], dst_ref=parts_in.at[slot],
                send_sem=rs_send.at[g], recv_sem=rs_recv,
                device_id=(me_s, owner(g)), device_id_type=MESH,
            ).start()

    @pl.when(jnp.logical_not(jnp.logical_or(first, tail)))
    def _():
        pl.semaphore_wait(ready.at[1], 1)
        send_rim(1)

    def finish_border(side):
        base = side * (nb - RIM)
        rim = pl.ds(side * nb, RIM)
        wait_for(rim_in.at[side], rim_recv.at[side])
        spread[rim] = (back[rim] + rim_in[side].astype(jnp.float32)).astype(jnp.bfloat16)
        for i in range(RIM):
            border[side, me_e, i] = forward(base + i)
        give_border(side)

    def give_border(side, order=partners):
        for p in order:
            pltpu.make_async_remote_copy(
                src_ref=border.at[side, me_e], dst_ref=border.at[side, me_e],
                send_sem=border_send.at[side], recv_sem=border_recv.at[side],
                device_id=(me_s, p), device_id_type=MESH,
            ).start()

    @pl.when(last)
    def _():
        pl.semaphore_wait(ready.at[0], 1)
        send_rim(0)

    near = 1 - lax.rem(me_s, 2)
    far = 1 - near
    finish_border(near)

    width = RIM * BS
    owns = jnp.logical_and(me_e >= owner(0), me_e < owner(inner))

    @pl.when(owns)
    def _():
        wait_for(parts_in, rs_recv)
        g = me_e - owner(0)
        total = part[g]
        for k in range(n_ens - 1):
            total = total + parts_in[k]
        mine = pl.ds(pl.multiple_of((g + 1) * width, width), width)
        out_ref[:, mine] = jnp.concatenate([total[i] for i in range(RIM)], axis=1)
        for p in partners:
            pltpu.make_async_remote_copy(
                src_ref=out_ref.at[:, mine], dst_ref=out_ref.at[:, mine],
                send_sem=ag_send, recv_sem=ag_recv.at[g],
                device_id=(me_s, p), device_id_type=MESH,
            ).start()

    @pl.when(first)
    def _():
        pl.semaphore_wait(ready.at[0], 1)
        send_rim(0)

    @pl.when(jnp.logical_not(first))
    def _():
        finish_border(far)

    @pl.when(taker)
    def _():
        def finish_row(r):
            wait_for(rims.at[r], rims_recv.at[r])

            if r > 0:
                for i, (mine, gift) in enumerate(gifts):
                    wait_for(gift.at[r - 1], gift_recv.at[i, r - 1])
                for b in range(RIM):
                    members[:, cells(b)] = gift_members[r - 1, b]
                spread[RIM : 2 * RIM] = gift_spread[r - 1]
                back[0:RIM] = gift_back[r - 1].astype(jnp.float32)

            spread[0:RIM] = (back[0:RIM] + rims[r].astype(jnp.float32)).astype(jnp.bfloat16)
            for i in range(RIM):
                if r == 0:
                    border[0, me_e, i] = forward(i)
                else:
                    border[0, me_e, i] += forward(i)

        for r in range(n_rows):
            finish_row(r)
        give_border(0, partners[ROW : 2 * ROW] + partners[2 * ROW :] + partners[:ROW])

    def sum_border(side, count=n_ens):
        total = border[side, 0]
        for k in range(1, count):
            total = total + border[side, k]
        columns = pl.ds(pl.multiple_of(side * (nb - RIM) * BS, width), width)
        out_ref[:, columns] = jnp.concatenate([total[i] for i in range(RIM)], axis=1)

    others = pl.ds(0, n_ens - 1)
    wait_for(border.at[near, others], border_recv.at[near])
    sum_border(near)
    wait_for(border.at[near, others], border_send.at[near])
    for g in range(inner):

        @pl.when(me_e != owner(g))
        def _():
            wait_for(out_ref.at[:, pl.ds((g + 1) * width, width)], ag_recv.at[g])
            wait_for(part.at[g], rs_send.at[g])

    @pl.when(owns)
    def _():
        wait_for(parts_in, ag_send)

    for side in (0, 1):
        wait_for(rim_out.at[side], rim_send.at[side])

    @pl.when(giver)
    def _():
        for i, (mine, gift) in enumerate(gifts):
            wait_for(gift.at[0], gift_send.at[i])
        wait_for(border.at[0, 0:ROW], border_recv.at[0])

    @pl.when(taker)
    def _():
        wait_for(border.at[0, 0 : ROW - 1], border_recv.at[0])

    @pl.when(first)
    def _():
        sum_border(0, ROW)

    @pl.when(taker)
    def _():
        wait_for(border.at[0, others], border_send.at[0])

    @pl.when(jnp.logical_not(first))
    def _():
        wait_for(border.at[far, others], border_recv.at[far])
        sum_border(far)
        wait_for(border.at[far, others], border_send.at[far])


def local(n_space, n_ens, members, field, weight, offsets):
    member_count, ch, cell_total = members.shape
    nb = weight.shape[0]
    rows = member_count * ch
    inner = nb // RIM - 2
    dma = pltpu.SemaphoreType.DMA
    call = pl.pallas_call(
        functools.partial(kernel, n_space, n_ens, nb, rows, ch),
        out_shape=pltpu.VMEM((ch, cell_total), jnp.float32),
        in_specs=[pl.BlockSpec(memory_space=pltpu.HBM)] * 4,
        out_specs=pl.BlockSpec(memory_space=pltpu.VMEM),
        scratch_shapes=[
            pltpu.SMEM((TAPS, nb), jnp.int32),
            pltpu.VMEM((rows, cell_total), jnp.bfloat16),
            pltpu.VMEM((ch, cell_total), jnp.bfloat16),
            pltpu.VMEM((nb, TAPS * BS, BS), jnp.bfloat16),
            pltpu.VMEM((nb + RIM, rows, BS), jnp.float32),
            pltpu.VMEM((nb + RIM, rows, BS), jnp.bfloat16),
            pltpu.VMEM((2, RIM, rows, BS), jnp.bfloat16),
            pltpu.VMEM((2, RIM, rows, BS), jnp.bfloat16),
            pltpu.VMEM((inner, RIM, ch, BS), jnp.float32),
            pltpu.VMEM((n_ens - 1, RIM, ch, BS), jnp.float32),
            pltpu.VMEM((2, n_ens, RIM, ch, BS), jnp.float32),
            pltpu.VMEM((n_ens // ROW, RIM, rows, BS), jnp.bfloat16),
            pltpu.VMEM((RIM, rows, BS), jnp.bfloat16),
            pltpu.VMEM((n_ens // ROW - 1, RIM, rows, BS), jnp.bfloat16),
            pltpu.VMEM((n_ens // ROW - 1, RIM, rows, BS), jnp.bfloat16),
            pltpu.VMEM((n_ens // ROW - 1, RIM, rows, BS), jnp.bfloat16),
            dma((3,)),
            dma((3,)),
            dma((nb // RIM,)),
            pltpu.SemaphoreType.REGULAR((2,)),
            pltpu.SemaphoreType.REGULAR,
            dma((2,)),
            dma((2,)),
            dma((inner,)),
            dma,
            dma,
            dma((inner,)),
            dma((2,)),
            dma((2,)),
            dma((n_ens // ROW,)),
            dma((3,)),
            dma((3, n_ens // ROW - 1)),
        ],
        compiler_params=pltpu.CompilerParams(
            collective_id=0, has_side_effects=True, vmem_limit_bytes=VMEM_LIMIT
        ),
        cost_estimate=pl.CostEstimate(flops=403_000_000, bytes_accessed=3_800_000, transcendentals=0),
    )
    operands = (
        offsets.T,
        members.reshape(rows, cell_total),
        field,
        weight.reshape(nb, TAPS * BS, BS),
    )
    return call(*(pltpu.with_memory_space_constraint(x, pltpu.HBM) for x in operands))


def solution(mesh):
    in_specs = (
        P("ens", None, "space"),
        P(None, "space"),
        P("space", None, None, None),
        P("space", None),
    )
    out_specs = P(None, "space")
    body = functools.partial(local, mesh.shape["space"], mesh.shape["ens"])
    return jax.shard_map(body, mesh=mesh, in_specs=in_specs, out_specs=out_specs, check_vma=False)
```

```python
import functools

import jax
import jax.numpy as jnp
from jax import lax
from jax.experimental import pallas as pl
from jax.experimental.pallas import tpu as pltpu
from jax.sharding import PartitionSpec as P

BS = 128
HALO = 2
TAPS = 4
RIM = 2 * HALO
ROW = 4
MESH = pl.DeviceIdType.MESH
VMEM_LIMIT = 32 * 1024 * 1024


def kernel(
    n_space, n_ens, nb, rows, ch,
    offsets_hbm, members_hbm, field_hbm, weight_hbm, out_ref,
    offsets, members, field, weight, back, spread, rim_out, rim_in, part, parts_in, border,
    rims, pack, gift_members, gift_spread, gift_back,
    in_sems, member_sems, weight_sems, ready, met, rim_send, rim_recv, rs_send, rs_recv, ag_send, ag_recv, border_send, border_recv,
    rims_recv, gift_send, gift_recv,
):
    me_s = lax.axis_index("space")
    me_e = lax.axis_index("ens")
    right = lax.rem(me_s + 1, n_space)
    left = lax.rem(me_s + n_space - 1, n_space)
    first = me_s == 0
    last = me_s == n_space - 1
    ends = jnp.logical_or(first, last)
    tail = me_s >= n_space - 2
    chunks = nb // RIM
    inner = chunks - 2
    order = [chunks - 1, 0] + list(range(1, chunks - 1))

    row, x = me_e // ROW, lax.rem(me_e, ROW)
    away = jnp.where(row == 0, 2, 1)
    partners = []
    for dz in (away, n_ens // ROW - away, 0):
        for dx in (2, 1, 3, 0):
            if dx or not isinstance(dz, int):
                partners.append(lax.rem(row + dz, n_ens // ROW) * ROW + lax.rem(x + dx, ROW))
    cross = [row * ROW + lax.rem(x + dx, ROW) for dx in range(1, ROW)]
    cross += [lax.rem(row + dz, n_ens // ROW) * ROW + x for dz in range(1, n_ens // ROW)]

    n_rows = n_ens // ROW
    giver = jnp.logical_and(first, row > 0)
    taker = jnp.logical_and(first, row == 0)

    def owner(g):
        return ROW + g

    loads = [
        pltpu.make_async_copy(offsets_hbm, offsets, in_sems.at[2]),
        pltpu.make_async_copy(field_hbm, field, in_sems.at[1]),
    ]
    for copy in loads:
        copy.start()
    member_copies, weight_copies = {}, {}
    pieces = {chunks - 1: (chunks - 1, chunks), 0: (0, 1), 1: (1, chunks - 1)}
    for c in order:
        if c in pieces:
            low, high = pieces[c]
            columns = pl.ds(low * RIM * BS, (high - low) * RIM * BS)
            member_copies[c] = pltpu.make_async_copy(members_hbm.at[:, columns], members.at[:, columns], member_sems.at[len(member_copies)])
        piece = pl.ds(c * RIM, RIM)
        weight_copies[c] = pltpu.make_async_copy(weight_hbm.at[piece], weight.at[piece], weight_sems.at[c])

    def load(c):
        if c in member_copies:
            member_copies[c].start()
        weight_copies[c].start()

    load(chunks - 1)
    load(0)

    barrier = pltpu.get_barrier_semaphore()

    @pl.when(jnp.logical_not(tail))
    def _():
        pl.semaphore_signal(barrier, inc=1, device_id=(right, me_e), device_id_type=MESH)

    @pl.when(ends)
    def _():
        pl.semaphore_signal(barrier, inc=1, device_id=(left, me_e), device_id_type=MESH)

    @pl.when(taker)
    def _():
        for r in range(1, n_rows):
            pl.semaphore_signal(barrier, inc=1, device_id=(left, r * ROW + x), device_id_type=MESH)

    for p in cross:
        pl.semaphore_signal(barrier, inc=1, device_id=(me_s, p), device_id_type=MESH)

    back[...] = jnp.zeros_like(back)

    def cells(b):
        return pl.ds(b * BS if isinstance(b, int) else pl.multiple_of(b * BS, BS), BS)

    def adjoint(b):
        m = members[:, cells(b)].astype(jnp.float32).reshape(rows // ch, ch, BS)
        f = field[:, cells(b)].astype(jnp.float32)
        scaled = (m * f[None]).astype(jnp.bfloat16).reshape(rows, BS)
        product = lax.dot_general(
            scaled, weight[b], (((1,), (1,)), ((), ())), preferred_element_type=jnp.float32
        )
        taps = [offsets[t, b] for t in range(TAPS)]
        for reach in range(-HALO, HALO + 1):
            slab = None
            for t in range(TAPS):
                term = jnp.where(taps[t] == reach, product[:, t * BS : (t + 1) * BS], 0.0)
                slab = term if slab is None else slab + term
            back[b + HALO + reach] += slab

    def forward(b):
        total = None
        for t in range(TAPS):
            source = spread[b + HALO + offsets[t, b]]
            term = jnp.dot(source, weight[b, t * BS : (t + 1) * BS, :], preferred_element_type=jnp.float32)
            total = term if total is None else total + term
        m = members[:, cells(b)].astype(jnp.float32).reshape(rows // ch, ch, BS)
        return jnp.sum(m * total.reshape(rows // ch, ch, BS), axis=0)

    def send_rim(side):
        pltpu.make_async_remote_copy(
            src_ref=rim_out.at[side], dst_ref=rim_in.at[1 - side],
            send_sem=rim_send.at[side], recv_sem=rim_recv.at[1 - side],
            device_id=(right if side else left, me_e), device_id_type=MESH,
        ).start()

    def wait_for(ref, sem):
        pltpu.make_async_copy(ref, ref, sem).wait()

    for copy in loads:
        copy.wait()
    member_copies[chunks - 1].wait()
    weight_copies[chunks - 1].wait()
    def load_inner():
        for c in order[2:]:
            load(c)

    pl.when(jnp.logical_not(last))(load_inner)
    for b in range(nb - RIM, nb):
        adjoint(b)
    rim_out[1] = back[nb : nb + RIM].astype(jnp.bfloat16)
    pl.semaphore_wait(barrier, len(cross) + jnp.where(ends, 0, 1) + jnp.where(tail, 1, 0)
        + jnp.where(jnp.logical_and(last, row > 0), 1, 0))

    @pl.when(tail)
    def _():
        @pl.when(last)
        def _():
            pltpu.make_async_remote_copy(
                src_ref=rim_out.at[1], dst_ref=rims.at[row],
                send_sem=rim_send.at[1], recv_sem=rims_recv.at[row],
                device_id=(right, x), device_id_type=MESH,
            ).start()

        @pl.when(jnp.logical_not(last))
        def _():
            send_rim(1)

        pl.semaphore_signal(ready.at[0], inc=1, device_id=(right, me_e), device_id_type=MESH)

    member_copies[0].wait()
    weight_copies[0].wait()
    for b in range(RIM):
        adjoint(b)
    rim_out[0] = back[0:RIM].astype(jnp.bfloat16)

    @pl.when(jnp.logical_not(ends))
    def _():
        send_rim(0)
        pl.semaphore_signal(ready.at[1], inc=1, device_id=(left, me_e), device_id_type=MESH)

    pl.when(last)(load_inner)

    for p in cross:
        pl.semaphore_signal(met, inc=1, device_id=(me_s, p), device_id_type=MESH)

    @pl.when(first)
    def _():
        pl.semaphore_wait(ready.at[1], 1)
        send_rim(1)

    gifts = (
        (pack, gift_members),
        (spread.at[RIM : 2 * RIM], gift_spread),
        (rim_out.at[0], gift_back),
    )

    @pl.when(giver)
    def _():
        for b in range(RIM):
            pack[b] = members[:, cells(b)]
        for i, (mine, gift) in ((0, gifts[0]), (2, gifts[2])):
            pltpu.make_async_remote_copy(
                src_ref=mine, dst_ref=gift.at[row - 1],
                send_sem=gift_send.at[i], recv_sem=gift_recv.at[i, row - 1],
                device_id=(me_s, x), device_id_type=MESH,
            ).start()

    for c in range(1, chunks - 1):
        if c in member_copies:
            member_copies[c].wait()
        weight_copies[c].wait()
        for b in range(c * RIM, (c + 1) * RIM):
            adjoint(b)

    spread[RIM:nb] = back[RIM:nb].astype(jnp.bfloat16)

    @pl.when(giver)
    def _():
        pltpu.make_async_remote_copy(
            src_ref=gifts[1][0], dst_ref=gift_spread.at[row - 1],
            send_sem=gift_send.at[1], recv_sem=gift_recv.at[1, row - 1],
            device_id=(me_s, x), device_id_type=MESH,
        ).start()

    pl.semaphore_wait(met, len(cross))
    for g in range(inner):
        for i in range(RIM):
            part[g, i] = forward(RIM * (g + 1) + i)

        @pl.when(me_e != owner(g))
        def _():
            slot = lax.rem(owner(g) - me_e + n_ens, n_ens) - 1
            pltpu.make_async_remote_copy(
                src_ref=part.at[g], dst_ref=parts_in.at[slot],
                send_sem=rs_send.at[g], recv_sem=rs_recv,
                device_id=(me_s, owner(g)), device_id_type=MESH,
            ).start()

    @pl.when(jnp.logical_not(jnp.logical_or(first, tail)))
    def _():
        pl.semaphore_wait(ready.at[1], 1)
        send_rim(1)

    def finish_border(side):
        base = side * (nb - RIM)
        rim = pl.ds(side * nb, RIM)
        wait_for(rim_in.at[side], rim_recv.at[side])
        spread[rim] = (back[rim] + rim_in[side].astype(jnp.float32)).astype(jnp.bfloat16)
        for i in range(RIM):
            border[side, me_e, i] = forward(base + i)
        give_border(side)

    def give_border(side, order=partners):
        for p in order:
            pltpu.make_async_remote_copy(
                src_ref=border.at[side, me_e], dst_ref=border.at[side, me_e],
                send_sem=border_send.at[side], recv_sem=border_recv.at[side],
                device_id=(me_s, p), device_id_type=MESH,
            ).start()

    @pl.when(last)
    def _():
        pl.semaphore_wait(ready.at[0], 1)
        send_rim(0)

    near = 1 - lax.rem(me_s, 2)
    far = 1 - near
    finish_border(near)

    width = RIM * BS
    owns = jnp.logical_and(me_e >= owner(0), me_e < owner(inner))

    @pl.when(owns)
    def _():
        wait_for(parts_in, rs_recv)
        g = me_e - owner(0)
        total = part[g]
        for k in range(n_ens - 1):
            total = total + parts_in[k]
        mine = pl.ds(pl.multiple_of((g + 1) * width, width), width)
        out_ref[:, mine] = jnp.concatenate([total[i] for i in range(RIM)], axis=1)
        for p in partners:
            pltpu.make_async_remote_copy(
                src_ref=out_ref.at[:, mine], dst_ref=out_ref.at[:, mine],
                send_sem=ag_send, recv_sem=ag_recv.at[g],
                device_id=(me_s, p), device_id_type=MESH,
            ).start()

    @pl.when(first)
    def _():
        pl.semaphore_wait(ready.at[0], 1)
        send_rim(0)

    @pl.when(jnp.logical_not(first))
    def _():
        finish_border(far)

    @pl.when(taker)
    def _():
        def finish_row(r):
            wait_for(rims.at[r], rims_recv.at[r])

            if r > 0:
                for i, (mine, gift) in enumerate(gifts):
                    wait_for(gift.at[r - 1], gift_recv.at[i, r - 1])
                for b in range(RIM):
                    members[:, cells(b)] = gift_members[r - 1, b]
                spread[RIM : 2 * RIM] = gift_spread[r - 1]
                back[0:RIM] = gift_back[r - 1].astype(jnp.float32)

            spread[0:RIM] = (back[0:RIM] + rims[r].astype(jnp.float32)).astype(jnp.bfloat16)
            for i in range(RIM):
                if r == 0:
                    border[0, me_e, i] = forward(i)
                else:
                    border[0, me_e, i] += forward(i)

        for r in range(n_rows):
            finish_row(r)
        give_border(0, partners[ROW : 2 * ROW] + partners[2 * ROW :] + partners[:ROW])

    def sum_border(side, count=n_ens):
        total = border[side, 0]
        for k in range(1, count):
            total = total + border[side, k]
        columns = pl.ds(pl.multiple_of(side * (nb - RIM) * BS, width), width)
        out_ref[:, columns] = jnp.concatenate([total[i] for i in range(RIM)], axis=1)

    others = pl.ds(0, n_ens - 1)
    wait_for(border.at[near, others], border_recv.at[near])
    sum_border(near)
    wait_for(border.at[near, others], border_send.at[near])
    for g in range(inner):

        @pl.when(me_e != owner(g))
        def _():
            wait_for(out_ref.at[:, pl.ds((g + 1) * width, width)], ag_recv.at[g])
            wait_for(part.at[g], rs_send.at[g])

    @pl.when(owns)
    def _():
        wait_for(parts_in, ag_send)

    for side in (0, 1):
        wait_for(rim_out.at[side], rim_send.at[side])

    @pl.when(giver)
    def _():
        for i, (mine, gift) in enumerate(gifts):
            wait_for(gift.at[0], gift_send.at[i])
        wait_for(border.at[0, 0:ROW], border_recv.at[0])

    @pl.when(taker)
    def _():
        wait_for(border.at[0, 0 : ROW - 1], border_recv.at[0])

    @pl.when(first)
    def _():
        sum_border(0, ROW)

    @pl.when(taker)
    def _():
        wait_for(border.at[0, others], border_send.at[0])

    @pl.when(jnp.logical_not(first))
    def _():
        wait_for(border.at[far, others], border_recv.at[far])
        sum_border(far)
        wait_for(border.at[far, others], border_send.at[far])


def local(n_space, n_ens, members, field, weight, offsets):
    member_count, ch, cell_total = members.shape
    nb = weight.shape[0]
    rows = member_count * ch
    inner = nb // RIM - 2
    dma = pltpu.SemaphoreType.DMA
    call = pl.pallas_call(
        functools.partial(kernel, n_space, n_ens, nb, rows, ch),
        out_shape=pltpu.VMEM((ch, cell_total), jnp.float32),
        in_specs=[pl.BlockSpec(memory_space=pltpu.HBM)] * 4,
        out_specs=pl.BlockSpec(memory_space=pltpu.VMEM),
        scratch_shapes=[
            pltpu.SMEM((TAPS, nb), jnp.int32),
            pltpu.VMEM((rows, cell_total), jnp.bfloat16),
            pltpu.VMEM((ch, cell_total), jnp.bfloat16),
            pltpu.VMEM((nb, TAPS * BS, BS), jnp.bfloat16),
            pltpu.VMEM((nb + RIM, rows, BS), jnp.float32),
            pltpu.VMEM((nb + RIM, rows, BS), jnp.bfloat16),
            pltpu.VMEM((2, RIM, rows, BS), jnp.bfloat16),
            pltpu.VMEM((2, RIM, rows, BS), jnp.bfloat16),
            pltpu.VMEM((inner, RIM, ch, BS), jnp.float32),
            pltpu.VMEM((n_ens - 1, RIM, ch, BS), jnp.float32),
            pltpu.VMEM((2, n_ens, RIM, ch, BS), jnp.float32),
            pltpu.VMEM((n_ens // ROW, RIM, rows, BS), jnp.bfloat16),
            pltpu.VMEM((RIM, rows, BS), jnp.bfloat16),
            pltpu.VMEM((n_ens // ROW - 1, RIM, rows, BS), jnp.bfloat16),
            pltpu.VMEM((n_ens // ROW - 1, RIM, rows, BS), jnp.bfloat16),
            pltpu.VMEM((n_ens // ROW - 1, RIM, rows, BS), jnp.bfloat16),
            dma((3,)),
            dma((3,)),
            dma((nb // RIM,)),
            pltpu.SemaphoreType.REGULAR((2,)),
            pltpu.SemaphoreType.REGULAR,
            dma((2,)),
            dma((2,)),
            dma((inner,)),
            dma,
            dma,
            dma((inner,)),
            dma((2,)),
            dma((2,)),
            dma((n_ens // ROW,)),
            dma((3,)),
            dma((3, n_ens // ROW - 1)),
        ],
        compiler_params=pltpu.CompilerParams(
            collective_id=0, has_side_effects=True, vmem_limit_bytes=VMEM_LIMIT
        ),
        cost_estimate=pl.CostEstimate(flops=403_000_000, bytes_accessed=3_800_000, transcendentals=0),
    )
    operands = (
        offsets.T,
        members.reshape(rows, cell_total),
        field,
        weight.reshape(nb, TAPS * BS, BS),
    )
    return call(*(pltpu.with_memory_space_constraint(x, pltpu.HBM) for x in operands))


def solution(mesh):
    in_specs = (
        P("ens", None, "space"),
        P(None, "space"),
        P("space", None, None, None),
        P("space", None),
    )
    out_specs = P(None, "space")
    body = functools.partial(local, mesh.shape["space"], mesh.shape["ens"])
    return jax.shard_map(body, mesh=mesh, in_specs=in_specs, out_specs=out_specs, check_vma=False)
```
